256 devices in a mesh: ex: 16 (over z, core), par: 16 (over y, x).
Axes of the slice: x: 4, y: 4, z: 8, core: 2. Of those that a mesh axis runs over, the one named last changes fastest.
Arguments:
- train_grads: bfloat16 [1024, 65536], P('ex', 'par')
- val_grads: bfloat16 [128, 65536], P('ex', 'par')
- token_counts: int32 [1024], P('ex'), may hold values from 128 to 511
- proj_salt: int32 [1], replicated, may hold values from 0 to 999999
Outputs:
- scores: float32 [1024, 128], P('ex', 'par')
- train_norm: float32 [1024], P('ex')
The draws below stay inside these ranges and needn't reach their ends.
All inputs are finite; a program needn't handle non-finite values.
Results may differ from the reference program's by a relative error of at most 0.0035.
Values may be sent and summed in bfloat16 or wider, within the bound.
A program may use at most 64 MiB of HBM per device.

```python
import jax
import jax.numpy as jnp
from jax import lax

K = 8192
P_DEV = 4096
P_SIZE = 65536
NTR = 1024
NVAL = 128


def shared_parts(key):
    return jax.random.normal(key, (2, P_SIZE), jnp.float32)


def mixed_grads(key, rows, common):
    coeff_key, noise_key = jax.random.split(key, 2)
    coeff = jax.random.normal(coeff_key, (rows, 2), jnp.float32)
    noise = jax.random.normal(noise_key, (rows, P_SIZE), jnp.float32)
    value = coeff[:, 0:1] * common[0][None, :] + coeff[:, 1:2] * common[1][None, :] + noise
    return value.astype(jnp.bfloat16)


def draw_train_grads(key, part):
    common = shared_parts(key)
    key = jax.random.fold_in(key, 11)
    return mixed_grads(key, NTR, common)


def draw_val_grads(key, part):
    common = shared_parts(key)
    key = jax.random.fold_in(key, 23)
    return mixed_grads(key, NVAL, common)


def set_ends(array, own_key, low, high):
    longest = array.shape.index(max(array.shape))
    spots = []
    for shift in (0, 1):
        where = [jax.random.randint(jax.random.fold_in(own_key, axis), (), 0, length) for axis, length in enumerate(array.shape)]
        where[longest] = (where[longest] + shift) % array.shape[longest]
        spots.append(tuple(where))
    return array.at[spots[0]].set(low).at[spots[1]].set(high)


def setup_inputs(seed: int = 0) -> dict:
    seeds = jax.random.split(jax.random.key(seed), 5)
    return {
        "train_grads": draw_train_grads(jax.random.fold_in(seeds[4], 71), 0),
        "val_grads": draw_val_grads(jax.random.fold_in(seeds[4], 71), 0),
        "token_counts": set_ends(jax.random.randint(seeds[2], (NTR,), 128, 512), jax.random.fold_in(seeds[2], 1), 128, 511).astype(jnp.int32),
        "proj_salt": jax.random.randint(seeds[3], (1,), 0, 1000000).astype(jnp.int32),
    }


def mixer(value, amount):
    return value ^ lax.shift_right_logical(value, jnp.full_like(value, amount))

def sign_block(row_ids, col_ids, salt_value):
    value = (row_ids[:, None] * K + col_ids[None, :]) * 625341585 + salt_value * 461845907
    value = mixer(value, 15)
    value = value * 739982445
    value = mixer(value, 12)
    value = value * 695872825
    value = mixer(value, 15)
    bit = lax.shift_right_logical(value, jnp.full_like(value, 16)) & 1
    return (1 - 2 * bit).astype(jnp.bfloat16)

def reference(train_grads, val_grads, token_counts, proj_salt):
    stacked = jnp.concatenate([train_grads, val_grads], axis=0)
    block_rows = min(512, P_DEV)
    col_ids = jnp.arange(K, dtype=jnp.int32)
    salt_value = proj_salt[0].astype(jnp.int32)

    def step(total, index):
        start = (index * block_rows).astype(jnp.int32)
        row_ids = start + jnp.arange(block_rows, dtype=jnp.int32)
        signs = sign_block(row_ids, col_ids, salt_value)
        piece = lax.dynamic_slice_in_dim(stacked, start, block_rows, 1)
        return (total + jnp.dot(piece, signs, preferred_element_type=jnp.float32), None)
    start_total = jnp.zeros((NTR + NVAL, K), jnp.float32)
    total, unused = lax.scan(step, start_total, jnp.arange(P_SIZE // block_rows, dtype=jnp.int32))
    projected = total * (1.0 / K ** 0.5)
    train_feat = projected[:NTR] / token_counts.astype(jnp.float32)[:, None]
    val_feat = projected[NTR:]
    train_norm = jnp.sqrt(lax.optimization_barrier(jnp.sum(train_feat * train_feat, axis=1)) + 1e-06)
    val_norm = jnp.sqrt(lax.optimization_barrier(jnp.sum(val_feat * val_feat, axis=1)) + 1e-06)
    inner = jnp.dot(train_feat, val_feat.T, precision=lax.Precision.HIGHEST, preferred_element_type=jnp.float32)
    scores = inner / (train_norm[:, None] * val_norm[None, :])
    return (scores, train_norm)
```

```python
import jax
import jax.numpy as jnp
from jax import lax
from jax.experimental import pallas as pl
from jax.experimental.pallas import tpu as pltpu
from jax.sharding import PartitionSpec as P

K = 8192
C1, C2, C3, CS = 625341585, 739982445, 695872825, 461845907
MESH = pl.DeviceIdType.MESH
NX = 4
NY = 4
NPAR = NX * NY
NZ = 8
NTR = 64
NVA = 8
NPAD = 80
ROWS = 2 * (NTR + NVA)
PD = 4096
KHALF = K // 2
KB = 512
NJ = KHALF // KB
QB = 1024
NB = PD // QB
NOWN = NJ // NY
SLAB = 16
ROOT = 1.0 / K**0.5


def wrap(value):
    value &= 0xFFFFFFFF
    return value - (1 << 32) if value >= (1 << 31) else value


def srl(value, amount):
    return lax.shift_right_logical(value, jnp.full_like(value, amount))


def signs_of(value):
    value = value ^ srl(value, 15)
    value = value * C2
    value = value ^ srl(value, 12)
    value = value * C3
    value = value ^ (value << 15)
    return jnp.where(value < 0, jnp.bfloat16(-1.0), jnp.bfloat16(1.0))


def dot_t(a, b):
    return lax.dot_general(a, b, (((1,), (1,)), ((), ())), preferred_element_type=jnp.float32)


def split_dot(a, b, exact):
    pair = (a, b)
    high = pair[exact].astype(jnp.bfloat16)
    low = (pair[exact] - high.astype(jnp.float32)).astype(jnp.bfloat16)
    if exact == 0:
        return dot_t(high, b) + dot_t(low, b)
    return dot_t(a, high) + dot_t(a, low)


def kernel(
    salt_ref, train_ref, val_ref, tokens_ref, scores_ref, norm_ref,
    grads, signs_a, signs_b, total, xsend, xrecv, ysend, yrecv, feats, vall,
    own, other, crecv, msg, precv,
    sem_g, sem_xs, sem_xr, sem_ys, sem_yr, sem_zs, sem_zr, sem_c, sem_ps, sem_pr,
):
    ex = lax.axis_index("ex")
    par = lax.axis_index("par")
    z, core = ex // 2, ex % 2
    y, x = par // NX, par % NX
    sibling = z * 2 + (1 - core)

    barrier = pltpu.get_barrier_semaphore()

    def greet(e, p):
        pl.semaphore_signal(barrier, inc=1, device_id=(e, p), device_id_type=MESH)

    greet(sibling, par)
    for d in range(1, NPAR):
        greet(ex, (par + d) % NPAR)
    for d in range(1, NZ):
        greet(((z + d) % NZ) * 2 + core, par)

    grads[core, 0:NTR, :] = train_ref[...]
    val_rows = val_ref[...].astype(jnp.float32)
    grads[core, NTR:NPAD, :] = jnp.concatenate([val_rows, jnp.zeros_like(val_rows)], axis=0).astype(jnp.bfloat16)

    base = (
        salt_ref[0] * CS
        + par * wrap(PD * K * C1)
        + core * wrap(KHALF * C1)
    )
    grid0 = (
        lax.broadcasted_iota(jnp.int32, (SLAB, KB), 0) * K
        + lax.broadcasted_iota(jnp.int32, (SLAB, KB), 1)
    ) * C1
    signs = (signs_a, signs_b)

    def make_signs(dst, j, b):
        first = wrap(j * KB * C1) if isinstance(j, int) else j * wrap(KB * C1)
        offset = base + first + wrap(b * QB * K * C1)
        for u in range(QB // SLAB):
            dst[u * SLAB : (u + 1) * SLAB, :] = signs_of(grid0 + (offset + wrap(u * SLAB * K * C1)))

    make_signs(signs_a, 0, 0)
    pl.semaphore_wait(barrier, 1 + (NPAR - 1) + (NZ - 1))

    share = pltpu.make_async_remote_copy(
        src_ref=grads.at[core], dst_ref=grads.at[core],
        send_sem=sem_g.at[0], recv_sem=sem_g.at[1],
        device_id=(sibling, par), device_id_type=MESH,
    )
    share.start()
    pltpu.make_async_remote_copy(
        src_ref=grads.at[1 - core], dst_ref=grads.at[1 - core],
        send_sem=sem_g.at[0], recv_sem=sem_g.at[1],
        device_id=(sibling, par), device_id_type=MESH,
    ).wait_recv()

    def x_copy(j, d):
        t = (x + d) % NX
        return pltpu.make_async_remote_copy(
            src_ref=xsend.at[j, t], dst_ref=xrecv.at[j, d - 1],
            send_sem=sem_xs.at[j, d - 1], recv_sem=sem_xr.at[j, d - 1],
            device_id=(ex, y * NX + t), device_id_type=MESH,
        )

    def y_copy(j, jj, d):
        return pltpu.make_async_remote_copy(
            src_ref=ysend.at[j], dst_ref=yrecv.at[jj, d - 1],
            send_sem=sem_ys.at[j], recv_sem=sem_yr.at[jj, d - 1],
            device_id=(ex, ((y + d) % NY) * NX + x), device_id_type=MESH,
        )

    def z_copy(jj, d):
        return pltpu.make_async_remote_copy(
            src_ref=vall.at[jj, z], dst_ref=vall.at[jj, z],
            send_sem=sem_zs.at[jj, d - 1], recv_sem=sem_zr.at[jj, d - 1],
            device_id=(((z + d) % NZ) * 2 + core, par), device_id_type=MESH,
        )

    def z_arrival(jj, d):
        source = (z + NZ - d) % NZ
        return pltpu.make_async_remote_copy(
            src_ref=vall.at[jj, source], dst_ref=vall.at[jj, source],
            send_sem=sem_zs.at[jj, d - 1], recv_sem=sem_zr.at[jj, d - 1],
            device_id=(source * 2 + core, par), device_id_type=MESH,
        )

    def p_copy(d):
        peer = (par + d) % NPAR
        return pltpu.make_async_remote_copy(
            src_ref=msg.at[peer], dst_ref=precv.at[d - 1],
            send_sem=sem_ps.at[d - 1], recv_sem=sem_pr.at[d - 1],
            device_id=(ex, peer), device_id_type=MESH,
        )

    def chunk(j, last):
        for b in range(NB):
            if b + 1 < NB:
                make_signs(signs[(b + 1) % 2], j, b + 1)
            elif not last:
                make_signs(signs[(b + 1) % 2], j + 1, 0)
            piece = grads[:, :, b * QB : (b + 1) * QB].reshape(2 * NPAD, QB)
            product = jnp.dot(piece, signs[b % 2][...], preferred_element_type=jnp.float32)
            if b == 0:
                total[...] = product
            else:
                total[...] += product
        for t in range(NX):
            lanes = slice(t * 128, (t + 1) * 128)
            xsend[j, t] = jnp.concatenate(
                [
                    total[0:NTR, lanes],
                    total[NPAD : NPAD + NTR, lanes],
                    total[NTR : NTR + NVA, lanes],
                    total[NPAD + NTR : NPAD + NTR + NVA, lanes],
                ],
                axis=0,
            ).astype(jnp.bfloat16)
        for d in range(1, NX):
            x_copy(j, d).start()

    def reduce_x(j):
        for d in range(1, NX):
            x_copy(j, d).wait_recv()
        tile = xsend[j, x].astype(jnp.float32)
        for d in range(1, NX):
            tile += xrecv[j, d - 1].astype(jnp.float32)
        owner, jj = j % NY, j // NY

        @pl.when(owner == y)
        def _():
            feats[jj] = tile

        for d in range(1, NY):

            @pl.when(owner == (y + d) % NY)
            def _():
                ysend[j] = tile.astype(jnp.bfloat16)
                y_copy(j, jj, d).start()

    def reduce_y(jj):
        for d in range(1, NY):
            y_copy(0, jj, d).wait_recv()
        tile = feats[jj]
        for d in range(1, NY):
            tile += yrecv[jj, d - 1].astype(jnp.float32)
        feats[jj] = tile
        vall[jj, z] = (tile[2 * NTR :] * ROOT).astype(jnp.bfloat16)
        for d in range(1, NZ):
            z_copy(jj, d).start()

    lane = lax.broadcasted_iota(jnp.int32, (128, 128), 1)
    row = lax.broadcasted_iota(jnp.int32, (128, 128), 0)
    ones = jnp.ones((128, 128), jnp.bfloat16)

    def products(jj):
        for d in range(1, NZ):
            z_arrival(jj, d).wait_recv()
        values = vall[jj].reshape(128, 128)
        square = values.astype(jnp.float32)
        val_sq = split_dot(square * square, ones, 0)
        out = []
        for half in (core, 1 - core):
            rows = feats[jj, pl.ds(pl.multiple_of(half * NTR, NTR), NTR), :] * (ROOT / 512.0)
            rows = jnp.concatenate([rows, rows], axis=0)
            inner = dot_t(values, rows.astype(jnp.bfloat16))
            train_sq = split_dot(ones, rows * rows, 1)
            sums = jnp.where(
                lane % 8 == row % 8,
                train_sq,
                jnp.where(lane % 8 == (row + 1) % 8, val_sq, 0.0),
            )
            out.append(jnp.where(lane < NTR, inner, sums))
        if jj == 0:
            own[...] = out[0]
            other[...] = out[1]
        else:
            own[...] += out[0]
            other[...] += out[1]

    @pl.loop(0, NJ - 1)
    def _(j):
        chunk(j, False)

        @pl.when(j >= 1)
        def _():
            reduce_x(j - 1)

        @pl.when(j == NY + 1)
        def _():
            reduce_y(0)

        @pl.when(j == NY + 2)
        def _():
            products(0)

    chunk(NJ - 1, True)
    reduce_x(NJ - 2)
    reduce_x(NJ - 1)
    reduce_y(NOWN - 1)
    products(NOWN - 1)

    swap = pltpu.make_async_remote_copy(
        src_ref=other, dst_ref=crecv, send_sem=sem_c.at[0], recv_sem=sem_c.at[1],
        device_id=(sibling, par), device_id_type=MESH,
    )
    swap.start()
    swap.wait_recv()
    msg[...] = (own[...] + crecv[...]).reshape(NPAR, 8, 128)
    for d in range(1, NPAR):
        p_copy(d).start()
    for d in range(1, NPAR):
        p_copy(d).wait_recv()
    result = msg[par]
    for d in range(1, NPAR):
        result += precv[d - 1]

    lane8 = lax.broadcasted_iota(jnp.int32, (8, 128), 1)
    row8 = lax.broadcasted_iota(jnp.int32, (8, 128), 0)
    train_sq = jnp.sum(jnp.where(lane8 % 8 == row8, result, 0.0), axis=0, keepdims=True)[:, NTR:]
    val_sq = 0.125 * jnp.sum(
        jnp.where((lane8 >= NTR) & (lane8 % 8 == (row8 + 1) % 8), result, 0.0), axis=1, keepdims=True
    )
    back = 512.0 / tokens_ref[...].astype(jnp.float32)
    train_norm = jnp.sqrt(train_sq * back * back + 1e-6)
    val_norm = jnp.sqrt(val_sq + 1e-6)
    norm_ref[...] = train_norm
    scores = result[:, :NTR] * back / (train_norm * val_norm)
    scores_ref[...] = scores.T

    share.wait_send()
    swap.wait_send()
    for d in range(1, NPAR):
        p_copy(d).wait_send()
    for jj in range(NOWN):
        for d in range(1, NZ):
            z_copy(jj, d).wait_send()

    @pl.loop(0, NJ)
    def _(j):
        for d in range(1, NX):
            x_copy(j, d).wait_send()

        @pl.when(j % NY != y)
        def _():
            y_copy(j, 0, 1).wait_send()


def local(train_grads, val_grads, token_counts, proj_salt):
    vmem = pl.BlockSpec(memory_space=pltpu.VMEM)
    dma = pltpu.SemaphoreType.DMA
    scores, norm = pl.pallas_call(
        kernel,
        out_shape=(
            jax.ShapeDtypeStruct((NTR, NVA), jnp.float32),
            jax.ShapeDtypeStruct((1, NTR), jnp.float32),
        ),
        in_specs=[pl.BlockSpec(memory_space=pltpu.SMEM), vmem, vmem, vmem],
        out_specs=(vmem, vmem),
        scratch_shapes=[
            pltpu.VMEM((2, NPAD, PD), jnp.bfloat16),
            pltpu.VMEM((QB, KB), jnp.bfloat16),
            pltpu.VMEM((QB, KB), jnp.bfloat16),
            pltpu.VMEM((2 * NPAD, KB), jnp.float32),
            pltpu.VMEM((NJ, NX, ROWS, 128), jnp.bfloat16),
            pltpu.VMEM((NJ, NX - 1, ROWS, 128), jnp.bfloat16),
            pltpu.VMEM((NJ, ROWS, 128), jnp.bfloat16),
            pltpu.VMEM((NOWN, NY - 1, ROWS, 128), jnp.bfloat16),
            pltpu.VMEM((NOWN, ROWS, 128), jnp.float32),
            pltpu.VMEM((NOWN, NZ, 16, 128), jnp.bfloat16),
            pltpu.VMEM((128, 128), jnp.float32),
            pltpu.VMEM((128, 128), jnp.float32),
            pltpu.VMEM((128, 128), jnp.float32),
            pltpu.VMEM((NPAR, 8, 128), jnp.float32),
            pltpu.VMEM((NPAR - 1, 8, 128), jnp.float32),
            dma((2,)),
            dma((NJ, NX - 1)),
            dma((NJ, NX - 1)),
            dma((NJ,)),
            dma((NOWN, NY - 1)),
            dma((NOWN, NZ - 1)),
            dma((NOWN, NZ - 1)),
            dma((2,)),
            dma((NPAR - 1,)),
            dma((NPAR - 1,)),
        ],
        compiler_params=pltpu.CompilerParams(
            collective_id=0, has_side_effects=True, vmem_limit_bytes=48 * 2**20
        ),
    )(proj_salt, train_grads, val_grads, token_counts.reshape(1, NTR))
    return scores, norm.reshape(NTR)


def solution(mesh):
    placed = (P("ex", "par"), P("ex", "par"), P("ex"), P())
    return jax.shard_map(
        local, mesh=mesh, in_specs=placed, out_specs=(P("ex", "par"), P("ex")), check_vma=False
    )
```

```python
import jax
import jax.numpy as jnp
from jax import lax
from jax.experimental import pallas as pl
from jax.experimental.pallas import tpu as pltpu
from jax.sharding import PartitionSpec as P

K = 8192
C1, C2, C3, CS = 625341585, 739982445, 695872825, 461845907
MESH = pl.DeviceIdType.MESH
NX = 4
NY = 4
NPAR = NX * NY
NZ = 8
NTR = 64
NVA = 8
HALF = NTR // 2
PD = 4096
KQ = K // 4
KB = 512
QB = 1024
NB = PD // QB
NPIECE = 2 * NB
R1, R2, R3 = 2 * NTR, 2 * HALF + 4 * NVA, 2 * HALF
SLAB = 16
ROOT = 1.0 / K**0.5


def wrap(value):
    value &= 0xFFFFFFFF
    return value - (1 << 32) if value >= (1 << 31) else value


def srl(value, amount):
    return lax.shift_right_logical(value, jnp.full_like(value, amount))


def signs_of(value):
    value = value ^ srl(value, 15)
    value = value * C2
    value = value ^ srl(value, 12)
    value = value * C3
    value = value ^ (value << 15)
    return jnp.where(value < 0, jnp.bfloat16(-1.0), jnp.bfloat16(1.0))


def dot_t(a, b):
    return lax.dot_general(a, b, (((1,), (1,)), ((), ())), preferred_element_type=jnp.float32)


def split_dot(a, b, exact):
    pair = (a, b)
    high = pair[exact].astype(jnp.bfloat16)
    low = (pair[exact] - high.astype(jnp.float32)).astype(jnp.bfloat16)
    if exact == 0:
        return dot_t(high, b) + dot_t(low, b)
    return dot_t(a, high) + dot_t(a, low)


def kernel(
    salt_ref, train_ref, val_ref, tokens_ref, scores_ref, norm_ref,
    loc, rem0, rem1, vpad, valp, signs0, signs1, signs2, signs3,
    acc1, acc2, acc3, snd1, snd2, snd3, rcv1, rcv2, rcv3,
    vall, qsend, qrecv, msg, precv,
    sem_share, sem_ts, sem_tr, sem_fs, sem_fr,
    ss1, rs1, ss2, rs2, ss3, rs3, sem_zs, sem_zr, sem_qs, sem_qr, sem_ps, sem_pr,
):
    ex = lax.axis_index("ex")
    par = lax.axis_index("par")
    z, core = ex // 2, ex % 2
    y, x = par // NX, par % NX
    side = z % 2
    partner = z + 1 - 2 * side
    sibling = z * 2 + (1 - core)
    across = partner * 2 + core
    slant = partner * 2 + (1 - core)
    signs = (signs0, signs1, signs2, signs3)
    rem = (rem0, rem1)

    barrier = pltpu.get_barrier_semaphore()

    def greet(e, p):
        pl.semaphore_signal(barrier, inc=1, device_id=(e, p), device_id_type=MESH)

    greet(across, par)
    greet(sibling, par)
    greet(slant, par)
    for d in range(1, NPAR):
        greet(ex, (par + d) % NPAR)
    for d in range(1, NZ // 2):
        greet(((z + 2 * d) % NZ) * 2 + core, par)

    loc[core] = train_ref[...]
    val_rows = val_ref[...].astype(jnp.float32)
    vpad[core] = jnp.concatenate([val_rows, jnp.zeros_like(val_rows)], axis=0).astype(jnp.bfloat16)

    base = (
        salt_ref[0] * CS
        + par * wrap(PD * K * C1)
        + (side * 2 + core) * wrap(KQ * C1)
    )
    grid0 = (
        lax.broadcasted_iota(jnp.int32, (SLAB, KB), 0) * K
        + lax.broadcasted_iota(jnp.int32, (SLAB, KB), 1)
    ) * C1

    def tiles_of(i):
        return (y + 1 + i) % NY

    def block_start(i, b):
        return base + tiles_of(i) * wrap(KB * C1) + b * wrap(QB * K * C1)

    def make_signs(i, b):
        start = block_start(i, b)
        first = pl.multiple_of(b * QB, QB)
        for u in range(QB // SLAB):
            signs[i][pl.ds(first + u * SLAB, SLAB), :] = signs_of(grid0 + (start + wrap(u * SLAB * K * C1)))

    def make_signs_alone(i, b):
        start = block_start(i, b)
        first = pl.multiple_of(b * QB, QB)

        @pl.loop(0, QB // (4 * SLAB))
        def _(v):
            for u in range(4):
                at = pl.multiple_of(first + (v * 4 + u) * SLAB, SLAB)
                offset = start + (v * 4 + u) * wrap(SLAB * K * C1)
                signs[i][pl.ds(at, SLAB), :] = signs_of(grid0 + offset)

    def lanes(b):
        if isinstance(b, int):
            return slice(b * QB, (b + 1) * QB)
        return pl.ds(pl.multiple_of(b * QB, QB), QB)

    def product(rows, i, b):
        return jnp.dot(rows, signs[i][lanes(b), :], preferred_element_type=jnp.float32)

    def rows1(b):
        return loc[:, :, lanes(b)].reshape(R1, QB)

    def rows2(b):
        values = valp[:, b // 2, :, pl.ds(pl.multiple_of((b % 2) * QB, QB), QB)].reshape(4 * NVA, QB)
        return jnp.concatenate([rem0[:, :, lanes(b)].reshape(2 * HALF, QB), values], axis=0)

    def rows3(b):
        return rem1[:, :, lanes(b)].reshape(R3, QB)

    def remote(src, dst, send, recv, e, p):
        return pltpu.make_async_remote_copy(
            src_ref=src, dst_ref=dst, send_sem=send, recv_sem=recv,
            device_id=(e, p), device_id_type=MESH,
        )

    def share_copy(n, ref, slot):
        return remote(ref.at[slot], ref.at[slot], sem_share.at[n], sem_share.at[n + 2], sibling, par)

    def t_copy(k):
        h, q = k // NB, k % NB
        return remote(
            loc.at[core, h * HALF : (h + 1) * HALF, lanes(q)], rem[h].at[core, :, lanes(q)],
            sem_ts.at[k], sem_tr.at[k], across, par,
        )

    def f_copy(k, h, q, slot):
        part = rem[h].at[slot, :, lanes(q)]
        return remote(part, part, sem_fs.at[k], sem_fr.at[k], sibling, par)

    def forward(k):
        t_copy(k).wait_recv()
        f_copy(k, k // NB, k % NB, core).start()

    def v_copy():
        part = valp.at[side, core]
        return remote(part, part, sem_ts.at[NPIECE], sem_tr.at[NPIECE], across, par)

    def vf_copy(slot):
        part = valp.at[1 - side, slot]
        return remote(part, part, sem_fs.at[NPIECE], sem_fr.at[NPIECE], sibling, par)

    def v_arrival():
        part = valp.at[1 - side, core]
        return remote(part, part, sem_ts.at[NPIECE], sem_tr.at[NPIECE], across, par)

    def scatter_copy(snd, rcv, send, recv, i, t, peer):
        d = (peer + NPAR - par) % NPAR
        return remote(snd.at[i, t], rcv.at[d - 1], send.at[d - 1], recv.at[d - 1], ex, peer)

    def scatter(value, i, snd, rcv, send, recv):
        for t in range(NX):
            snd[i, t] = value[:, t * 128 : (t + 1) * 128].astype(jnp.bfloat16)
        if i < NY - 1:
            for t in range(NX):
                scatter_copy(snd, rcv, send, recv, i, t, tiles_of(i) * NX + t).start()
        else:
            for d in range(1, NX):
                t = (x + d) % NX
                scatter_copy(snd, rcv, send, recv, i, t, y * NX + t).start()

    def scatter_wait(snd, rcv, send, recv, d):
        return remote(snd.at[0, 0], rcv.at[d - 1], send.at[d - 1], recv.at[d - 1], ex, (par + d) % NPAR)

    def gathered(snd, rcv, send, recv):
        for d in range(1, NPAR):
            scatter_wait(snd, rcv, send, recv, d).wait_recv()
        tile = snd[NY - 1, x].astype(jnp.float32)
        for d in range(1, NPAR):
            tile += rcv[d - 1].astype(jnp.float32)
        return tile

    pass1 = (snd1, rcv1, ss1, rs1)
    pass2 = (snd2, rcv2, ss2, rs2)
    pass3 = (snd3, rcv3, ss3, rs3)

    def z_copy(d):
        peer = (z + 2 * d) % NZ
        part = vall.at[z // 2]
        return remote(part, part, sem_zs.at[d - 1], sem_zr.at[d - 1], peer * 2 + core, par)

    def z_arrival(d):
        source = (z + NZ - 2 * d) % NZ
        part = vall.at[source // 2]
        return remote(part, part, sem_zs.at[d - 1], sem_zr.at[d - 1], source * 2 + core, par)

    def q_copy(n):
        src = (qsend.at[0, 1 - core], qsend.at[1, core], qsend.at[1, 1 - core])[n]
        return remote(src, qrecv.at[n], sem_qs.at[n], sem_qr.at[n], (sibling, across, slant)[n], par)

    def p_copy(d):
        peer = (par + d) % NPAR
        return remote(msg.at[peer], precv.at[d - 1], sem_ps.at[d - 1], sem_pr.at[d - 1], ex, peer)

    @pl.loop(0, NB)
    def _(b):
        make_signs_alone(0, b)

    pl.semaphore_wait(barrier, 3 + (NPAR - 1) + (NZ // 2 - 1))
    share_copy(0, vpad, core).start()
    t_copy(0).start()
    share_copy(1, loc, core).start()

    @pl.loop(0, 2)
    def _(b):
        make_signs_alone(1, b)

    share_copy(0, vpad, 1 - core).wait_recv()
    own_val = jnp.concatenate(
        [vpad[0].astype(jnp.float32)[:NVA], vpad[1].astype(jnp.float32)[:NVA]], axis=0
    ).astype(jnp.bfloat16)
    valp[side, 0] = own_val[:, : PD // 2]
    valp[side, 1] = own_val[:, PD // 2 :]
    v_copy().start()
    t_copy(1).start()
    t_copy(2).start()
    share_copy(1, loc, 1 - core).wait_recv()

    acc1[...] = jnp.zeros_like(acc1)

    @pl.loop(0, 2)
    def _(b):
        make_signs(1, b + 2)
        acc1[...] += product(rows1(2 * b), 0, 2 * b) + product(rows1(2 * b + 1), 0, 2 * b + 1)

    scatter(acc1, 0, *pass1)
    t_copy(3).start()
    forward(0)

    acc1[...] = jnp.zeros_like(acc1)

    @pl.loop(0, NB)
    def _(b):
        make_signs(2, b)
        acc1[...] += product(rows1(b), 1, b)

        @pl.when(b == 1)
        def _():
            t_copy(4).start()
            v_arrival().wait_recv()
            vf_copy(core).start()

        @pl.when(b == 2)
        def _():
            forward(1)

    scatter(acc1, 1, *pass1)
    t_copy(5).start()
    forward(2)

    acc1[...] = jnp.zeros_like(acc1)
    acc2[...] = jnp.zeros_like(acc2)
    vf_copy(1 - core).wait_recv()

    @pl.loop(0, NB)
    def _(b):
        f_copy(b, 0, b, 1 - core).wait_recv()
        make_signs(3, b)
        acc1[...] += product(rows1(b), 2, b)
        both = rows2(b)
        for i in range(NY - 1):
            acc2[i] += product(both, i, b)

        @pl.when(b == 0)
        def _():
            t_copy(6).start()

        @pl.when(b == 1)
        def _():
            forward(3)

        @pl.when(b == 2)
        def _():
            t_copy(7).start()

    scatter(acc1, 2, *pass1)
    for i in range(NY - 1):
        scatter(acc2.at[i], i, *pass2)
    forward(4)

    acc1[...] = jnp.zeros_like(acc1)
    acc3[...] = jnp.zeros_like(acc3)

    @pl.loop(0, NB)
    def _(b):
        acc1[...] += product(rows1(b), 3, b)
        acc2[3] += product(rows2(b), 3, b)

    scatter(acc1, 3, *pass1)
    scatter(acc2.at[3], 3, *pass2)
    forward(5)

    @pl.loop(0, NB)
    def _(b):
        f_copy(NB + b, 1, b, 1 - core).wait_recv()
        for i in range(NY):
            acc3[i] += product(rows3(b), i, b)

        @pl.when(b == 0)
        def _():
            forward(6)

        @pl.when(b == 1)
        def _():
            forward(7)

    for i in range(NY):
        scatter(acc3.at[i], i, *pass3)

    second = gathered(*pass2)
    vall[z // 2] = (second[2 * HALF :] * ROOT).astype(jnp.bfloat16)
    for d in range(1, NZ // 2):
        z_copy(d).start()

    lane = lax.broadcasted_iota(jnp.int32, (128, 128), 1)
    row = lax.broadcasted_iota(jnp.int32, (128, 128), 0)
    ones = jnp.ones((128, 128), jnp.bfloat16)

    first = gathered(*pass1)
    for d in range(1, NZ // 2):
        z_arrival(d).wait_recv()
    values = vall[...].reshape(128, 128)
    square = values.astype(jnp.float32)
    val_sq = split_dot(square * square, ones, 0)

    def products(rows, chip):
        rows = rows * (ROOT / 512.0)
        inner = dot_t(values, rows.astype(jnp.bfloat16))
        train_sq = pltpu.roll(split_dot(ones, rows * rows, 1), NTR, 1)
        sums = jnp.where(
            lane % 8 == row % 8,
            train_sq,
            jnp.where(lane % 8 == (row + 1) % 8, val_sq, 0.0),
        )
        pair = jnp.where(lane < NTR, inner, sums), jnp.where(lane < NTR, sums, inner)
        qsend[chip, 0] = pair[0].astype(jnp.bfloat16)
        qsend[chip, 1] = pair[1].astype(jnp.bfloat16)

    products(first, 0)
    q_copy(0).start()
    third = gathered(*pass3)
    products(
        jnp.concatenate([second[:HALF], third[:HALF], second[HALF : 2 * HALF], third[HALF:]], axis=0), 1
    )
    q_copy(1).start()
    q_copy(2).start()
    whole = qsend[0, core].astype(jnp.float32)
    for n in range(3):
        q_copy(n).wait_recv()
        whole += qrecv[n].astype(jnp.float32)
    msg[...] = whole.reshape(NPAR, 8, 128)
    for d in range(1, NPAR):
        p_copy(d).start()
    for d in range(1, NPAR):
        p_copy(d).wait_recv()
    result = msg[par]
    for d in range(1, NPAR):
        result += precv[d - 1]
    result = jnp.where(core == 1, pltpu.roll(result, NTR, 1), result)

    lane8 = lax.broadcasted_iota(jnp.int32, (8, 128), 1)
    row8 = lax.broadcasted_iota(jnp.int32, (8, 128), 0)
    train_sq = jnp.sum(jnp.where(lane8 % 8 == row8, result, 0.0), axis=0, keepdims=True)[:, NTR:]
    val_sq = 0.125 * jnp.sum(
        jnp.where((lane8 >= NTR) & (lane8 % 8 == (row8 + 1) % 8), result, 0.0), axis=1, keepdims=True
    )
    back = 512.0 / tokens_ref[...].astype(jnp.float32)
    train_norm = jnp.sqrt(train_sq * back * back + 1e-6)
    val_norm = jnp.sqrt(val_sq + 1e-6)
    norm_ref[...] = train_norm
    scores = result[:, :NTR] * back / (train_norm * val_norm)
    scores_ref[...] = scores.T

    for n, ref in enumerate((vpad, loc)):
        share_copy(n, ref, core).wait_send()
    for k in range(NPIECE):
        t_copy(k).wait_send()
        f_copy(k, k // NB, k % NB, core).wait_send()
    v_copy().wait_send()
    vf_copy(core).wait_send()
    for d in range(1, NPAR):
        for group in (pass1, pass2, pass3):
            scatter_wait(*group, d).wait_send()
        p_copy(d).wait_send()
    for d in range(1, NZ // 2):
        z_copy(d).wait_send()
    for n in range(3):
        q_copy(n).wait_send()


def local(train_grads, val_grads, token_counts, proj_salt):
    vmem = pl.BlockSpec(memory_space=pltpu.VMEM)
    dma = pltpu.SemaphoreType.DMA
    bf16, f32 = jnp.bfloat16, jnp.float32
    scores, norm = pl.pallas_call(
        kernel,
        out_shape=(
            jax.ShapeDtypeStruct((NTR, NVA), f32),
            jax.ShapeDtypeStruct((1, NTR), f32),
        ),
        in_specs=[pl.BlockSpec(memory_space=pltpu.SMEM), vmem, vmem, vmem],
        out_specs=(vmem, vmem),
        scratch_shapes=[
            pltpu.VMEM((2, NTR, PD), bf16),
            pltpu.VMEM((2, HALF, PD), bf16),
            pltpu.VMEM((2, HALF, PD), bf16),
            pltpu.VMEM((2, 2 * NVA, PD), bf16),
            pltpu.VMEM((2, 2, 2 * NVA, PD // 2), bf16),
            pltpu.VMEM((PD, KB), bf16),
            pltpu.VMEM((PD, KB), bf16),
            pltpu.VMEM((PD, KB), bf16),
            pltpu.VMEM((PD, KB), bf16),
            pltpu.VMEM((R1, KB), f32),
            pltpu.VMEM((NY, R2, KB), f32),
            pltpu.VMEM((NY, R3, KB), f32),
            pltpu.VMEM((NY, NX, R1, 128), bf16),
            pltpu.VMEM((NY, NX, R2, 128), bf16),
            pltpu.VMEM((NY, NX, R3, 128), bf16),
            pltpu.VMEM((NPAR - 1, R1, 128), bf16),
            pltpu.VMEM((NPAR - 1, R2, 128), bf16),
            pltpu.VMEM((NPAR - 1, R3, 128), bf16),
            pltpu.VMEM((NZ // 2, 4 * NVA, 128), bf16),
            pltpu.VMEM((2, 2, 128, 128), bf16),
            pltpu.VMEM((3, 128, 128), bf16),
            pltpu.VMEM((NPAR, 8, 128), f32),
            pltpu.VMEM((NPAR - 1, 8, 128), f32),
            dma((4,)),
            dma((NPIECE + 1,)),
            dma((NPIECE + 1,)),
            dma((NPIECE + 1,)),
            dma((NPIECE + 1,)),
            dma((NPAR - 1,)),
            dma((NPAR - 1,)),
            dma((NPAR - 1,)),
            dma((NPAR - 1,)),
            dma((NPAR - 1,)),
            dma((NPAR - 1,)),
            dma((NZ // 2 - 1,)),
            dma((NZ // 2 - 1,)),
            dma((3,)),
            dma((3,)),
            dma((NPAR - 1,)),
            dma((NPAR - 1,)),
        ],
        compiler_params=pltpu.CompilerParams(
            collective_id=0, has_side_effects=True, vmem_limit_bytes=52 * 2**20
        ),
    )(proj_salt, train_grads, val_grads, token_counts.reshape(1, NTR))
    return scores, norm.reshape(NTR)


def solution(mesh):
    placed = (P("ex", "par"), P("ex", "par"), P("ex"), P())
    return jax.shard_map(
        local, mesh=mesh, in_specs=placed, out_specs=(P("ex", "par"), P("ex")), check_vma=False
    )
```

```python
import jax
import jax.numpy as jnp
from jax import lax
from jax.experimental import pallas as pl
from jax.experimental.pallas import tpu as pltpu
from jax.sharding import PartitionSpec as P

K = 8192
C1, C2, C3, CS = 625341585, 739982445, 695872825, 461845907
MESH = pl.DeviceIdType.MESH
NX = 4
NY = 4
NPAR = NX * NY
NZ = 8
NTR = 64
NVA = 8
PD = 4096
KQ = K // 4
KB = 512
QB = 1024
NB = PD // QB
NPIECE = 8
QP = PD // NPIECE
HALF = PD // 2
R1, R2 = 2 * NTR + 4 * NVA, 2 * NTR
SLAB = 16
UNROLL = 32
ROOT = 1.0 / K**0.5


def wrap(value):
    value &= 0xFFFFFFFF
    return value - (1 << 32) if value >= (1 << 31) else value


def srl(value, amount):
    return lax.shift_right_logical(value, jnp.full_like(value, amount))


def signs_of(value):
    value = value ^ srl(value, 15)
    value = value * C2
    value = value ^ srl(value, 12)
    value = value * C3
    value = value ^ (value << 15)
    return jnp.where(value < 0, jnp.bfloat16(-1.0), jnp.bfloat16(1.0))


def dot_t(a, b):
    return lax.dot_general(a, b, (((1,), (1,)), ((), ())), preferred_element_type=jnp.float32)


def split_dot(a, b, exact):
    pair = (a, b)
    high = pair[exact].astype(jnp.bfloat16)
    low = (pair[exact] - high.astype(jnp.float32)).astype(jnp.bfloat16)
    if exact == 0:
        return dot_t(high, b) + dot_t(low, b)
    return dot_t(a, high) + dot_t(a, low)


def kernel(
    salt_ref, train_ref, val_ref, tokens_ref, scores_ref, norm_ref,
    salt, tokens, val_in, loc, rem, vpad, valp, signs,
    acc, snd1, snd2, rcv1, rcv2,
    vall, qsend, qrecv, msg, precv,
    sem_in, sem_share, sem_ts, sem_tr, sem_fs, sem_fr,
    ss1, rs1, ss2, rs2, sem_zs, sem_zr, sem_qs, sem_qr, sem_ps, sem_pr,
):
    ex = lax.axis_index("ex")
    par = lax.axis_index("par")
    z, core = ex // 2, ex % 2
    y, x = par // NX, par % NX
    side = z % 2
    partner = z + 1 - 2 * side
    sibling = z * 2 + (1 - core)
    across = partner * 2 + core
    slant = partner * 2 + (1 - core)

    barrier = pltpu.get_barrier_semaphore()

    def greet(e, p):
        pl.semaphore_signal(barrier, inc=1, device_id=(e, p), device_id_type=MESH)

    greet(across, par)
    greet(sibling, par)
    greet(slant, par)
    for d in range(1, NPAR):
        greet(ex, (par + d) % NPAR)
    for d in range(1, NZ // 2):
        greet(((z + 2 * d) % NZ) * 2 + core, par)

    arrivals = [
        pltpu.make_async_copy(src, dst, sem_in.at[n])
        for n, (src, dst) in enumerate(
            ((salt_ref, salt), (val_ref, val_in), (train_ref, loc.at[core]), (tokens_ref, tokens))
        )
    ]
    for arrival in arrivals:
        arrival.start()

    arrivals[0].wait()
    base = (
        salt[0] * CS
        + par * wrap(PD * K * C1)
        + (side * 2 + core) * wrap(KQ * C1)
    )
    grid0 = (
        lax.broadcasted_iota(jnp.int32, (SLAB, KB), 0) * K
        + lax.broadcasted_iota(jnp.int32, (SLAB, KB), 1)
    ) * C1

    def tiles_of(i):
        return (y + 1 + i) % NY

    def make_signs(n):
        i, b = n // NB, n % NB
        start = base + tiles_of(i) * wrap(KB * C1) + b * wrap(QB * K * C1)

        @pl.loop(0, QB // (UNROLL * SLAB))
        def _(v):
            here = start + v * wrap(UNROLL * SLAB * K * C1)
            for u in range(UNROLL):
                at = pl.multiple_of(b * QB + (v * UNROLL + u) * SLAB, SLAB)
                signs[i, pl.ds(at, SLAB), :] = signs_of(grid0 + (here + wrap(u * SLAB * K * C1)))

    def product1(i):
        values = [valp[:, h].reshape(4 * NVA, HALF) for h in range(2)]
        rows = jnp.concatenate([loc[...].reshape(2 * NTR, PD), jnp.concatenate(values, axis=1)], axis=0)
        return jnp.dot(rows, signs[i], preferred_element_type=jnp.float32)

    def product2(i, h):
        part = slice(h * HALF, (h + 1) * HALF)
        rows = rem[:, :, part].reshape(R2, HALF)
        return jnp.dot(rows, signs[i, part, :], preferred_element_type=jnp.float32)

    def remote(src, dst, send, recv, e, p):
        return pltpu.make_async_remote_copy(
            src_ref=src, dst_ref=dst, send_sem=send, recv_sem=recv,
            device_id=(e, p), device_id_type=MESH,
        )

    def share_copy(n, ref, slot):
        return remote(ref.at[slot], ref.at[slot], sem_share.at[n], sem_share.at[n + 2], sibling, par)

    def t_copy(k):
        part = slice(k * QP, (k + 1) * QP)
        return remote(
            loc.at[core, :, part], rem.at[core, :, part], sem_ts.at[k], sem_tr.at[k], across, par
        )

    def f_copy(k, slot):
        part = rem.at[slot, :, k * QP : (k + 1) * QP]
        return remote(part, part, sem_fs.at[k], sem_fr.at[k], sibling, par)

    def forward(k):
        t_copy(k).wait_recv()
        f_copy(k, core).start()

    def v_copy():
        part = valp.at[side, core]
        return remote(part, part, sem_ts.at[NPIECE], sem_tr.at[NPIECE], across, par)

    def vf_copy(slot):
        part = valp.at[1 - side, slot]
        return remote(part, part, sem_fs.at[NPIECE], sem_fr.at[NPIECE], sibling, par)

    def v_arrival():
        part = valp.at[1 - side, core]
        return remote(part, part, sem_ts.at[NPIECE], sem_tr.at[NPIECE], across, par)

    def scatter_copy(snd, rcv, send, recv, i, t, peer):
        d = (peer + NPAR - par) % NPAR
        return remote(snd.at[i, t], rcv.at[d - 1], send.at[d - 1], recv.at[d - 1], ex, peer)

    def scatter(value, i, snd, rcv, send, recv):
        for t in range(NX):
            snd[i, t] = value[:, t * 128 : (t + 1) * 128].astype(jnp.bfloat16)
        for d in range(NX):
            t = (x + d) % NX
            peer = tiles_of(i) * NX + t

            @pl.when(peer != par)
            def _():
                scatter_copy(snd, rcv, send, recv, i, t, peer).start()

    def scatter_wait(snd, rcv, send, recv, d):
        return remote(snd.at[0, 0], rcv.at[d - 1], send.at[d - 1], recv.at[d - 1], ex, (par + d) % NPAR)

    def gathered(snd, rcv, send, recv):
        for d in range(1, NPAR):
            scatter_wait(snd, rcv, send, recv, d).wait_recv()
        tile = snd[NY - 1, x].astype(jnp.float32)
        for d in range(1, NPAR):
            tile += rcv[d - 1].astype(jnp.float32)
        return tile

    pass1 = (snd1, rcv1, ss1, rs1)
    pass2 = (snd2, rcv2, ss2, rs2)

    def z_copy(d):
        peer = (z + 2 * d) % NZ
        part = vall.at[z // 2]
        return remote(part, part, sem_zs.at[d - 1], sem_zr.at[d - 1], peer * 2 + core, par)

    def z_arrival(d):
        source = (z + NZ - 2 * d) % NZ
        part = vall.at[source // 2]
        return remote(part, part, sem_zs.at[d - 1], sem_zr.at[d - 1], source * 2 + core, par)

    def q_copy(n):
        src = (qsend.at[0, 1 - core], qsend.at[1, core], qsend.at[1, 1 - core])[n]
        return remote(src, qrecv.at[n], sem_qs.at[n], sem_qr.at[n], (sibling, across, slant)[n], par)

    def p_copy(d):
        peer = (par + d) % NPAR
        return remote(msg.at[peer], precv.at[d - 1], sem_ps.at[d - 1], sem_pr.at[d - 1], ex, peer)

    def enter():
        arrivals[1].wait()
        val_rows = val_in[...].astype(jnp.float32)
        vpad[core] = jnp.concatenate([val_rows, jnp.zeros_like(val_rows)], axis=0).astype(jnp.bfloat16)
        arrivals[2].wait()
        arrivals[3].wait()
        pl.semaphore_wait(barrier, 3 + (NPAR - 1) + (NZ // 2 - 1))
        share_copy(0, vpad, core).start()
        t_copy(0).start()
        share_copy(1, loc, core).start()

    def send_val():
        share_copy(0, vpad, 1 - core).wait_recv()
        own_val = jnp.concatenate(
            [vpad[0].astype(jnp.float32)[:NVA], vpad[1].astype(jnp.float32)[:NVA]], axis=0
        ).astype(jnp.bfloat16)
        valp[side, 0] = own_val[:, :HALF]
        valp[side, 1] = own_val[:, HALF:]
        v_copy().start()

    def forward_val():
        v_arrival().wait_recv()
        vf_copy(core).start()

    def shared():
        vf_copy(1 - core).wait_recv()
        share_copy(1, loc, 1 - core).wait_recv()

    events = {
        1: [enter],
        3: [send_val, lambda: t_copy(1).start()],
        5: [lambda: t_copy(2).start()],
        7: [lambda: t_copy(3).start(), lambda: forward(0)],
        8: [lambda: t_copy(4).start(), forward_val],
        9: [lambda: t_copy(5).start(), shared],
        10: [lambda: t_copy(6).start(), lambda: forward(1)],
        11: [lambda: t_copy(7).start(), lambda: forward(2), lambda: forward(3)],
        13: [lambda: forward(4)],
        14: [lambda: forward(5)],
        15: [lambda: forward(6)],
    }

    @pl.loop(0, NY * NB)
    def _(n):
        make_signs(n)
        for when, things in events.items():

            @pl.when(n == when)
            def _():
                for thing in things:
                    thing()

        @pl.when((n == 9) | (n == 10) | (n == 12) | (n == 15))
        def _():
            i = jnp.where(n < 12, n - 9, jnp.where(n == 12, 2, 3))
            scatter(product1(i), i, *pass1)

    forward(7)

    for k in range(NPIECE // 2):
        f_copy(k, 1 - core).wait_recv()

    @pl.loop(0, NY)
    def _(i):
        acc[i] = product2(i, 0)

    for k in range(NPIECE // 2, NPIECE):
        f_copy(k, 1 - core).wait_recv()

    @pl.loop(0, NY)
    def _(i):
        scatter(acc[i] + product2(i, 1), i, *pass2)

    first = gathered(*pass1)
    vall[z // 2] = (first[2 * NTR :] * ROOT).astype(jnp.bfloat16)
    for d in range(1, NZ // 2):
        z_copy(d).start()

    lane = lax.broadcasted_iota(jnp.int32, (128, 128), 1)
    row = lax.broadcasted_iota(jnp.int32, (128, 128), 0)
    ones = jnp.ones((128, 128), jnp.bfloat16)

    for d in range(1, NZ // 2):
        z_arrival(d).wait_recv()
    values = vall[...].reshape(128, 128)
    square = values.astype(jnp.float32)
    val_sq = split_dot(square * square, ones, 0)

    def products(rows, chip):
        rows = rows * (ROOT / 512.0)
        inner = dot_t(values, rows.astype(jnp.bfloat16))
        train_sq = pltpu.roll(split_dot(ones, rows * rows, 1), NTR, 1)
        sums = jnp.where(
            lane % 8 == row % 8,
            train_sq,
            jnp.where(lane % 8 == (row + 1) % 8, val_sq, 0.0),
        )
        pair = jnp.where(lane < NTR, inner, sums), jnp.where(lane < NTR, sums, inner)
        qsend[chip, 0] = pair[0].astype(jnp.bfloat16)
        qsend[chip, 1] = pair[1].astype(jnp.bfloat16)

    products(first[: 2 * NTR], 0)
    q_copy(0).start()
    products(gathered(*pass2), 1)
    q_copy(1).start()
    q_copy(2).start()
    whole = qsend[0, core].astype(jnp.float32)
    for n in range(3):
        q_copy(n).wait_recv()
        whole += qrecv[n].astype(jnp.float32)
    msg[...] = whole.reshape(NPAR, 8, 128)
    for d in range(1, NPAR):
        p_copy(d).start()
    for d in range(1, NPAR):
        p_copy(d).wait_recv()
    result = msg[par]
    for d in range(1, NPAR):
        result += precv[d - 1]
    result = jnp.where(core == 1, pltpu.roll(result, NTR, 1), result)

    lane8 = lax.broadcasted_iota(jnp.int32, (8, 128), 1)
    row8 = lax.broadcasted_iota(jnp.int32, (8, 128), 0)
    train_sq = jnp.sum(jnp.where(lane8 % 8 == row8, result, 0.0), axis=0, keepdims=True)[:, NTR:]
    val_sq = 0.125 * jnp.sum(
        jnp.where((lane8 >= NTR) & (lane8 % 8 == (row8 + 1) % 8), result, 0.0), axis=1, keepdims=True
    )
    back = 512.0 / tokens[...].astype(jnp.float32)
    train_norm = jnp.sqrt(train_sq * back * back + 1e-6)
    val_norm = jnp.sqrt(val_sq + 1e-6)
    norm_ref[...] = train_norm
    scores = result[:, :NTR] * back / (train_norm * val_norm)
    scores_ref[...] = scores.T

    for n, ref in enumerate((vpad, loc)):
        share_copy(n, ref, core).wait_send()
    for k in range(NPIECE):
        t_copy(k).wait_send()
        f_copy(k, core).wait_send()
    v_copy().wait_send()
    vf_copy(core).wait_send()
    for d in range(1, NPAR):
        for group in (pass1, pass2):
            scatter_wait(*group, d).wait_send()
        p_copy(d).wait_send()
    for d in range(1, NZ // 2):
        z_copy(d).wait_send()
    for n in range(3):
        q_copy(n).wait_send()


def local(train_grads, val_grads, token_counts, proj_salt):
    vmem = pl.BlockSpec(memory_space=pltpu.VMEM)
    dma = pltpu.SemaphoreType.DMA
    bf16, f32 = jnp.bfloat16, jnp.float32
    scores, norm = pl.pallas_call(
        kernel,
        out_shape=(
            jax.ShapeDtypeStruct((NTR, NVA), f32),
            jax.ShapeDtypeStruct((1, NTR), f32),
        ),
        in_specs=[pl.BlockSpec(memory_space=pltpu.HBM)] * 4,
        out_specs=(vmem, vmem),
        scratch_shapes=[
            pltpu.SMEM((1,), jnp.int32),
            pltpu.VMEM((1, NTR), jnp.int32),
            pltpu.VMEM((NVA, PD), bf16),
            pltpu.VMEM((2, NTR, PD), bf16),
            pltpu.VMEM((2, NTR, PD), bf16),
            pltpu.VMEM((2, 2 * NVA, PD), bf16),
            pltpu.VMEM((2, 2, 2 * NVA, PD // 2), bf16),
            pltpu.VMEM((NY, PD, KB), bf16),
            pltpu.VMEM((NY, R2, KB), f32),
            pltpu.VMEM((NY, NX, R1, 128), bf16),
            pltpu.VMEM((NY, NX, R2, 128), bf16),
            pltpu.VMEM((NPAR - 1, R1, 128), bf16),
            pltpu.VMEM((NPAR - 1, R2, 128), bf16),
            pltpu.VMEM((NZ // 2, 4 * NVA, 128), bf16),
            pltpu.VMEM((2, 2, 128, 128), bf16),
            pltpu.VMEM((3, 128, 128), bf16),
            pltpu.VMEM((NPAR, 8, 128), f32),
            pltpu.VMEM((NPAR - 1, 8, 128), f32),
            dma((4,)),
            dma((4,)),
            dma((NPIECE + 1,)),
            dma((NPIECE + 1,)),
            dma((NPIECE + 1,)),
            dma((NPIECE + 1,)),
            dma((NPAR - 1,)),
            dma((NPAR - 1,)),
            dma((NPAR - 1,)),
            dma((NPAR - 1,)),
            dma((NZ // 2 - 1,)),
            dma((NZ // 2 - 1,)),
            dma((3,)),
            dma((3,)),
            dma((NPAR - 1,)),
            dma((NPAR - 1,)),
        ],
        compiler_params=pltpu.CompilerParams(
            collective_id=0, has_side_effects=True, vmem_limit_bytes=52 * 2**20
        ),
    )(proj_salt, train_grads, val_grads, token_counts.reshape(1, NTR))
    return scores, norm.reshape(NTR)


def solution(mesh):
    placed = (P("ex", "par"), P("ex", "par"), P("ex"), P())
    return jax.shard_map(
        local, mesh=mesh, in_specs=placed, out_specs=(P("ex", "par"), P("ex")), check_vma=False
    )
```

```python
import jax
import jax.numpy as jnp
from jax import lax
from jax.experimental import pallas as pl
from jax.experimental.pallas import tpu as pltpu
from jax.sharding import PartitionSpec as P

K = 8192
C1, C2, C3, CS = 625341585, 739982445, 695872825, 461845907
MESH = pl.DeviceIdType.MESH
NX = 4
NY = 4
NPAR = NX * NY
NZ = 8
NTR = 64
NVA = 8
PD = 4096
KQ = K // 4
KB = 512
QB = 1024
NB = PD // QB
NPIECE = 8
QP = PD // NPIECE
HALF = PD // 2
R1, R2 = 2 * NTR + 4 * NVA, 2 * NTR
SLAB = 16
UNROLL = 32
ROOT = 1.0 / K**0.5
ORDER = (
    ((2, 2), (1, 2), (3, 2), (2, 0)),
    ((2, 1), (2, 3), (0, 2), (1, 1)),
    ((3, 3), (1, 3), (3, 1), (0, 1)),
    ((0, 0), (0, 3), (1, 0), (3, 0)),
)


def wrap(value):
    value &= 0xFFFFFFFF
    return value - (1 << 32) if value >= (1 << 31) else value


def srl(value, amount):
    return lax.shift_right_logical(value, jnp.full_like(value, amount))


def signs_of(value):
    value = value ^ srl(value, 15)
    value = value * C2
    value = value ^ srl(value, 12)
    value = value * C3
    value = value ^ (value << 15)
    return jnp.where(value < 0, jnp.bfloat16(-1.0), jnp.bfloat16(1.0))


def dot_t(a, b):
    return lax.dot_general(a, b, (((1,), (1,)), ((), ())), preferred_element_type=jnp.float32)


def split_dot(a, b, exact):
    pair = (a, b)
    high = pair[exact].astype(jnp.bfloat16)
    low = (pair[exact] - high.astype(jnp.float32)).astype(jnp.bfloat16)
    if exact == 0:
        return dot_t(high, b) + dot_t(low, b)
    return dot_t(a, high) + dot_t(a, low)


def kernel(
    salt_ref, train_ref, val_ref, tokens_ref, scores_ref, norm_ref,
    salt, tokens, val_in, loc, rem, vpad, valp, signs,
    snd1, snd2, rcv1, rcv2,
    vall, qsend, qrecv, msg, precv,
    sem_in, sem_share, sem_ts, sem_tr, sem_fs, sem_fr,
    ss1, rs1, ss2, rs2, sem_zs, sem_zr, sem_qs, sem_qr, sem_ps, sem_pr,
):
    ex = lax.axis_index("ex")
    par = lax.axis_index("par")
    z, core = ex // 2, ex % 2
    y, x = par // NX, par % NX
    side = z % 2
    partner = z + 1 - 2 * side
    sibling = z * 2 + (1 - core)
    across = partner * 2 + core
    slant = partner * 2 + (1 - core)

    arrivals = [
        pltpu.make_async_copy(src, dst, sem_in.at[n])
        for n, (src, dst) in enumerate(
            ((salt_ref, salt), (val_ref, val_in), (train_ref, loc.at[core]), (tokens_ref, tokens))
        )
    ]
    for arrival in arrivals:
        arrival.start()

    barrier = pltpu.get_barrier_semaphore()

    def greet(e, p):
        pl.semaphore_signal(barrier, inc=1, device_id=(e, p), device_id_type=MESH)

    greet(across, par)
    greet(sibling, par)
    greet(slant, par)
    for d in range(1, NPAR):
        greet(ex, (par + d) % NPAR)
    for d in range(1, NZ // 2):
        greet(((z + 2 * d) % NZ) * 2 + core, par)

    arrivals[0].wait()
    base = (
        salt[0] * CS
        + par * wrap(PD * K * C1)
        + (side * 2 + core) * wrap(KQ * C1)
    )
    grid0 = (
        lax.broadcasted_iota(jnp.int32, (SLAB, 128), 0) * K
        + lax.broadcasted_iota(jnp.int32, (SLAB, 128), 1)
    ) * C1

    def owner(i, t):
        def pick(axis):
            value = ORDER[NY - 1][t][axis]
            for j in range(NY - 1):
                value = jnp.where(i == j, ORDER[j][t][axis], value)
            return value

        return ((y + pick(0)) % NY) * NX + (x + pick(1)) % NX

    def make_signs(n):
        i, b = n // NB, n % NB
        start = base + b * wrap(QB * K * C1)
        grid = jnp.concatenate([grid0 + (start + owner(i, t) * wrap(128 * C1)) for t in range(NX)], axis=1)

        @pl.loop(0, QB // (UNROLL * SLAB))
        def _(v):
            here = v * wrap(UNROLL * SLAB * K * C1)
            for u in range(UNROLL):
                at = pl.multiple_of(b * QB + (v * UNROLL + u) * SLAB, SLAB)
                signs[i, pl.ds(at, SLAB), :] = signs_of(grid + (here + wrap(u * SLAB * K * C1)))

    def product1(i):
        values = [valp[:, h].reshape(4 * NVA, HALF) for h in range(2)]
        rows = jnp.concatenate([loc[...].reshape(2 * NTR, PD), jnp.concatenate(values, axis=1)], axis=0)
        return jnp.dot(rows, signs[i], preferred_element_type=jnp.float32)

    def product2(i):
        return jnp.dot(rem[...].reshape(R2, PD), signs[i], preferred_element_type=jnp.float32)

    def remote(src, dst, send, recv, e, p):
        return pltpu.make_async_remote_copy(
            src_ref=src, dst_ref=dst, send_sem=send, recv_sem=recv,
            device_id=(e, p), device_id_type=MESH,
        )

    def share_copy(n, ref, slot):
        return remote(ref.at[slot], ref.at[slot], sem_share.at[n], sem_share.at[n + 2], sibling, par)

    def t_copy(k):
        part = slice(k * QP, (k + 1) * QP)
        return remote(
            loc.at[core, :, part], rem.at[core, :, part], sem_ts.at[k], sem_tr.at[k], across, par
        )

    def f_copy(k, slot):
        part = rem.at[slot, :, k * QP : (k + 1) * QP]
        return remote(part, part, sem_fs.at[k], sem_fr.at[k], sibling, par)

    def forward(k):
        t_copy(k).wait_recv()
        f_copy(k, core).start()

    def v_copy():
        part = valp.at[side, core]
        return remote(part, part, sem_ts.at[NPIECE], sem_tr.at[NPIECE], across, par)

    def vf_copy(slot):
        part = valp.at[1 - side, slot]
        return remote(part, part, sem_fs.at[NPIECE], sem_fr.at[NPIECE], sibling, par)

    def v_arrival():
        part = valp.at[1 - side, core]
        return remote(part, part, sem_ts.at[NPIECE], sem_tr.at[NPIECE], across, par)

    def scatter_copy(snd, rcv, send, recv, i, t, peer):
        d = (peer + NPAR - par) % NPAR
        return remote(snd.at[i, t], rcv.at[d - 1], send.at[d - 1], recv.at[d - 1], ex, peer)

    def scatter(value, i, snd, rcv, send, recv):
        for t in range(NX):
            snd[i, t] = value[:, t * 128 : (t + 1) * 128].astype(jnp.bfloat16)
        for t in range(NX):

            def send_tile():
                scatter_copy(snd, rcv, send, recv, i, t, owner(i, t)).start()

            if t:
                send_tile()
            else:
                pl.when(i < NY - 1)(send_tile)

    def scatter_wait(snd, rcv, send, recv, d):
        return remote(snd.at[0, 0], rcv.at[d - 1], send.at[d - 1], recv.at[d - 1], ex, (par + d) % NPAR)

    def gathered(snd, rcv, send, recv):
        for d in range(1, NPAR):
            scatter_wait(snd, rcv, send, recv, d).wait_recv()
        tile = snd[NY - 1, 0].astype(jnp.float32)
        for d in range(1, NPAR):
            tile += rcv[d - 1].astype(jnp.float32)
        return tile

    pass1 = (snd1, rcv1, ss1, rs1)
    pass2 = (snd2, rcv2, ss2, rs2)

    def z_copy(d):
        peer = (z + 2 * d) % NZ
        part = vall.at[z // 2]
        return remote(part, part, sem_zs.at[d - 1], sem_zr.at[d - 1], peer * 2 + core, par)

    def z_arrival(d):
        source = (z + NZ - 2 * d) % NZ
        part = vall.at[source // 2]
        return remote(part, part, sem_zs.at[d - 1], sem_zr.at[d - 1], source * 2 + core, par)

    def q_copy(n):
        src = (qsend.at[0, 1 - core], qsend.at[1, core], qsend.at[1, 1 - core])[n]
        return remote(src, qrecv.at[n], sem_qs.at[n], sem_qr.at[n], (sibling, across, slant)[n], par)

    def p_copy(d):
        peer = (par + d) % NPAR
        return remote(msg.at[peer], precv.at[d - 1], sem_ps.at[d - 1], sem_pr.at[d - 1], ex, peer)

    def enter():
        arrivals[1].wait()
        val_rows = val_in[...].astype(jnp.float32)
        vpad[core] = jnp.concatenate([val_rows, jnp.zeros_like(val_rows)], axis=0).astype(jnp.bfloat16)
        arrivals[2].wait()
        arrivals[3].wait()
        pl.semaphore_wait(barrier, 3 + (NPAR - 1) + (NZ // 2 - 1))
        share_copy(0, vpad, core).start()
        t_copy(0).start()
        share_copy(1, loc, core).start()

    def send_val():
        share_copy(0, vpad, 1 - core).wait_recv()
        own_val = jnp.concatenate(
            [vpad[0].astype(jnp.float32)[:NVA], vpad[1].astype(jnp.float32)[:NVA]], axis=0
        ).astype(jnp.bfloat16)
        valp[side, 0] = own_val[:, :HALF]
        valp[side, 1] = own_val[:, HALF:]
        v_copy().start()

    def forward_val():
        v_arrival().wait_recv()
        vf_copy(core).start()

    def shared():
        vf_copy(1 - core).wait_recv()
        share_copy(1, loc, 1 - core).wait_recv()

    events = {
        3: [enter],
        5: [send_val, lambda: t_copy(1).start(), lambda: t_copy(2).start()],
        7: [lambda: t_copy(3).start(), lambda: t_copy(4).start()],
        9: [lambda: t_copy(5).start(), lambda: forward(0), forward_val],
        10: [lambda: t_copy(6).start(), shared],
        11: [lambda: t_copy(7).start(), lambda: forward(1), lambda: forward(2)],
        12: [lambda: forward(3)],
        14: [lambda: forward(4)],
        15: [lambda: forward(5), lambda: forward(6)],
    }

    def own_rows(n):
        i = jnp.where(n < 12, n - 10, jnp.where(n < 15, 2, 3))
        scatter(product1(i), i, *pass1)

    def after(n, low, high):
        if not any(low <= when < high for when in events):
            return
        if high - low == 1:
            for thing in events[low]:
                thing()
            return
        middle = (low + high) // 2

        @pl.when(n < middle)
        def _():
            after(n, low, middle)

        @pl.when(n >= middle)
        def _():
            after(n, middle, high)

    @pl.loop(0, NY * NB)
    def _(n):
        make_signs(n)
        after(n, 0, NY * NB)

        @pl.when((n == 10) | (n == 11) | (n == 12) | (n == 15))
        def _():
            own_rows(n)

    forward(7)

    for k in range(NPIECE):
        f_copy(k, 1 - core).wait_recv()

    @pl.loop(0, NY)
    def _(i):
        scatter(product2(i), i, *pass2)

    first = gathered(*pass1)
    vall[z // 2] = (first[2 * NTR :] * ROOT).astype(jnp.bfloat16)
    for d in range(1, NZ // 2):
        z_copy(d).start()

    lane = lax.broadcasted_iota(jnp.int32, (128, 128), 1)
    row = lax.broadcasted_iota(jnp.int32, (128, 128), 0)
    ones = jnp.ones((128, 128), jnp.bfloat16)

    for d in range(1, NZ // 2):
        z_arrival(d).wait_recv()
    values = vall[...].reshape(128, 128)
    square = values.astype(jnp.float32)
    val_sq = split_dot(square * square, ones, 0)

    def products(rows, chip):
        rows = rows * (ROOT / 512.0)
        inner = dot_t(values, rows.astype(jnp.bfloat16))
        train_sq = pltpu.roll(split_dot(ones, rows * rows, 1), NTR, 1)
        sums = jnp.where(
            lane % 8 == row % 8,
            train_sq,
            jnp.where(lane % 8 == (row + 1) % 8, val_sq, 0.0),
        )
        pair = jnp.where(lane < NTR, inner, sums), jnp.where(lane < NTR, sums, inner)
        qsend[chip, 0] = pair[0].astype(jnp.bfloat16)
        qsend[chip, 1] = pair[1].astype(jnp.bfloat16)

    products(first[: 2 * NTR], 0)
    q_copy(0).start()
    products(gathered(*pass2), 1)
    q_copy(1).start()
    q_copy(2).start()
    whole = qsend[0, core].astype(jnp.float32)
    for n in range(3):
        q_copy(n).wait_recv()
        whole += qrecv[n].astype(jnp.float32)
    msg[...] = whole.reshape(NPAR, 8, 128)
    for d in range(1, NPAR):
        p_copy(d).start()
    for d in range(1, NPAR):
        p_copy(d).wait_recv()
    result = msg[par]
    for d in range(1, NPAR):
        result += precv[d - 1]
    result = jnp.where(core == 1, pltpu.roll(result, NTR, 1), result)

    lane8 = lax.broadcasted_iota(jnp.int32, (8, 128), 1)
    row8 = lax.broadcasted_iota(jnp.int32, (8, 128), 0)
    train_sq = jnp.sum(jnp.where(lane8 % 8 == row8, result, 0.0), axis=0, keepdims=True)[:, NTR:]
    val_sq = 0.125 * jnp.sum(
        jnp.where((lane8 >= NTR) & (lane8 % 8 == (row8 + 1) % 8), result, 0.0), axis=1, keepdims=True
    )
    back = 512.0 / tokens[...].astype(jnp.float32)
    train_norm = jnp.sqrt(train_sq * back * back + 1e-6)
    val_norm = jnp.sqrt(val_sq + 1e-6)
    norm_ref[...] = train_norm
    scores = result[:, :NTR] * back / (train_norm * val_norm)
    scores_ref[...] = scores.T

    for n, ref in enumerate((vpad, loc)):
        share_copy(n, ref, core).wait_send()
    for k in range(NPIECE):
        t_copy(k).wait_send()
        f_copy(k, core).wait_send()
    v_copy().wait_send()
    vf_copy(core).wait_send()
    for d in range(1, NPAR):
        for group in (pass1, pass2):
            scatter_wait(*group, d).wait_send()
        p_copy(d).wait_send()
    for d in range(1, NZ // 2):
        z_copy(d).wait_send()
    for n in range(3):
        q_copy(n).wait_send()


def local(train_grads, val_grads, token_counts, proj_salt):
    vmem = pl.BlockSpec(memory_space=pltpu.VMEM)
    dma = pltpu.SemaphoreType.DMA
    bf16, f32 = jnp.bfloat16, jnp.float32
    scores, norm = pl.pallas_call(
        kernel,
        out_shape=(
            jax.ShapeDtypeStruct((NTR, NVA), f32),
            jax.ShapeDtypeStruct((1, NTR), f32),
        ),
        in_specs=[pl.BlockSpec(memory_space=pltpu.HBM)] * 4,
        out_specs=(vmem, vmem),
        scratch_shapes=[
            pltpu.SMEM((1,), jnp.int32),
            pltpu.VMEM((1, NTR), jnp.int32),
            pltpu.VMEM((NVA, PD), bf16),
            pltpu.VMEM((2, NTR, PD), bf16),
            pltpu.VMEM((2, NTR, PD), bf16),
            pltpu.VMEM((2, 2 * NVA, PD), bf16),
            pltpu.VMEM((2, 2, 2 * NVA, PD // 2), bf16),
            pltpu.VMEM((NY, PD, KB), bf16),
            pltpu.VMEM((NY, NX, R1, 128), bf16),
            pltpu.VMEM((NY, NX, R2, 128), bf16),
            pltpu.VMEM((NPAR - 1, R1, 128), bf16),
            pltpu.VMEM((NPAR - 1, R2, 128), bf16),
            pltpu.VMEM((NZ // 2, 4 * NVA, 128), bf16),
            pltpu.VMEM((2, 2, 128, 128), bf16),
            pltpu.VMEM((3, 128, 128), bf16),
            pltpu.VMEM((NPAR, 8, 128), f32),
            pltpu.VMEM((NPAR - 1, 8, 128), f32),
            dma((4,)),
            dma((4,)),
            dma((NPIECE + 1,)),
            dma((NPIECE + 1,)),
            dma((NPIECE + 1,)),
            dma((NPIECE + 1,)),
            dma((NPAR - 1,)),
            dma((NPAR - 1,)),
            dma((NPAR - 1,)),
            dma((NPAR - 1,)),
            dma((NZ // 2 - 1,)),
            dma((NZ // 2 - 1,)),
            dma((3,)),
            dma((3,)),
            dma((NPAR - 1,)),
            dma((NPAR - 1,)),
        ],
        compiler_params=pltpu.CompilerParams(
            collective_id=0, has_side_effects=True, vmem_limit_bytes=52 * 2**20
        ),
    )(proj_salt, train_grads, val_grads, token_counts.reshape(1, NTR))
    return scores, norm.reshape(NTR)


def solution(mesh):
    placed = (P("ex", "par"), P("ex", "par"), P("ex"), P())
    return jax.shard_map(
        local, mesh=mesh, in_specs=placed, out_specs=(P("ex", "par"), P("ex")), check_vma=False
    )
```

```python
import jax
import jax.numpy as jnp
from jax import lax
from jax.experimental import pallas as pl
from jax.experimental.pallas import tpu as pltpu
from jax.sharding import PartitionSpec as P

K = 8192
C1, C2, C3, CS = 625341585, 739982445, 695872825, 461845907
MESH = pl.DeviceIdType.MESH
NX = 4
NY = 4
NPAR = NX * NY
NZ = 8
NTR = 64
NVA = 8
PD = 4096
KQ = K // 4
KB = 512
QB = 1024
NB = PD // QB
NPIECE = 8
QP = PD // NPIECE
HALF = PD // 2
R1, R2 = 2 * NTR + 4 * NVA, 2 * NTR
SLAB = 16
UNROLL = 32
ROOT = 1.0 / K**0.5
ORDER = (
    ((2, 2), (1, 2), (3, 2), (2, 0)),
    ((2, 1), (2, 3), (0, 2), (1, 1)),
    ((3, 3), (1, 3), (3, 1), (0, 1)),
    ((0, 0), (0, 3), (1, 0), (3, 0)),
)


def wrap(value):
    value &= 0xFFFFFFFF
    return value - (1 << 32) if value >= (1 << 31) else value


def srl(value, amount):
    return lax.shift_right_logical(value, jnp.full_like(value, amount))


def signs_of(value):
    value = value ^ srl(value, 15)
    value = value * C2
    value = value ^ srl(value, 12)
    value = value * C3
    value = value ^ (value << 15)
    return jnp.where(value < 0, jnp.bfloat16(-1.0), jnp.bfloat16(1.0))


def dot_t(a, b):
    return lax.dot_general(a, b, (((1,), (1,)), ((), ())), preferred_element_type=jnp.float32)


def split_dot(a, b, exact):
    pair = (a, b)
    high = pair[exact].astype(jnp.bfloat16)
    low = (pair[exact] - high.astype(jnp.float32)).astype(jnp.bfloat16)
    if exact == 0:
        return dot_t(high, b) + dot_t(low, b)
    return dot_t(a, high) + dot_t(a, low)


def kernel(
    salt_ref, train_ref, val_ref, tokens_ref, scores_ref, norm_ref,
    salt, tokens, val_in, loc, rem, vpad, valp, signs,
    snd1, snd2, rcv1, rcv2,
    vall, qsend, qrecv, msg, precv,
    sem_ready, sem_in, sem_share, sem_ts, sem_tr, sem_fs, sem_fr,
    ss1, rs1, ss2, rs2, sem_zs, sem_zr, sem_qs, sem_qr, sem_ps, sem_pr,
):
    ex = lax.axis_index("ex")
    par = lax.axis_index("par")
    z, core = ex // 2, ex % 2
    y, x = par // NX, par % NX
    side = z % 2
    partner = z + 1 - 2 * side
    sibling = z * 2 + (1 - core)
    across = partner * 2 + core
    slant = partner * 2 + (1 - core)

    arrivals = [
        pltpu.make_async_copy(src, dst, sem_in.at[n])
        for n, (src, dst) in enumerate(
            ((salt_ref, salt), (val_ref, val_in), (train_ref, loc.at[core]), (tokens_ref, tokens))
        )
    ]
    for arrival in arrivals:
        arrival.start()

    barrier = pltpu.get_barrier_semaphore()

    def greet(e, p):
        pl.semaphore_signal(barrier, inc=1, device_id=(e, p), device_id_type=MESH)

    row = [(ex, y * NX + (x + d) % NX) for d in (1, NX - 1)]
    column = [(ex, ((y + d) % NY) * NX + x) for d in (1, NY - 1)]
    stack = [(((z + d) % NZ) * 2 + core, par) for d in (1, NZ - 1)]
    greet(sibling, par)
    for e, p in stack + row + column:
        greet(e, p)


    arrivals[0].wait()
    base = (
        salt[0] * CS
        + par * wrap(PD * K * C1)
        + (side * 2 + core) * wrap(KQ * C1)
    )
    grid0 = (
        lax.broadcasted_iota(jnp.int32, (SLAB, 128), 0) * K
        + lax.broadcasted_iota(jnp.int32, (SLAB, 128), 1)
    ) * C1

    def offset(i, t):
        def pick(axis):
            value = ORDER[NY - 1][t][axis]
            for j in range(NY - 1):
                value = jnp.where(i == j, ORDER[j][t][axis], value)
            return value

        return pick(0), pick(1)

    def owner(i, t):
        dy, dx = offset(i, t)
        return ((y + dy) % NY) * NX + (x + dx) % NX

    def make_signs(n):
        i, b = n // NB, n % NB
        start = base + b * wrap(QB * K * C1)
        grid = jnp.concatenate([grid0 + (start + owner(i, t) * wrap(128 * C1)) for t in range(NX)], axis=1)

        @pl.loop(0, QB // (UNROLL * SLAB))
        def _(v):
            here = v * wrap(UNROLL * SLAB * K * C1)
            for u in range(UNROLL):
                at = pl.multiple_of(b * QB + (v * UNROLL + u) * SLAB, SLAB)
                signs[i, pl.ds(at, SLAB), :] = signs_of(grid + (here + wrap(u * SLAB * K * C1)))

    def product1(i):
        values = [valp[:, h].reshape(4 * NVA, HALF) for h in range(2)]
        rows = jnp.concatenate([loc[...].reshape(2 * NTR, PD), jnp.concatenate(values, axis=1)], axis=0)
        return jnp.dot(rows, signs[i], preferred_element_type=jnp.float32)

    def product2(i):
        return jnp.dot(rem[...].reshape(R2, PD), signs[i], preferred_element_type=jnp.float32)

    def remote(src, dst, send, recv, e, p):
        return pltpu.make_async_remote_copy(
            src_ref=src, dst_ref=dst, send_sem=send, recv_sem=recv,
            device_id=(e, p), device_id_type=MESH,
        )

    def share_copy(n, ref, slot):
        return remote(ref.at[slot], ref.at[slot], sem_share.at[n], sem_share.at[n + 2], sibling, par)

    def t_copy(k):
        part = slice(k * QP, (k + 1) * QP)
        return remote(
            loc.at[core, :, part], rem.at[core, :, part], sem_ts.at[k], sem_tr.at[k], across, par
        )

    def f_copy(k, slot):
        part = rem.at[slot, :, k * QP : (k + 1) * QP]
        return remote(part, part, sem_fs.at[k], sem_fr.at[k], sibling, par)

    def forward(k):
        t_copy(k).wait_recv()
        f_copy(k, core).start()

    def v_copy():
        part = valp.at[side, core]
        return remote(part, part, sem_ts.at[NPIECE], sem_tr.at[NPIECE], across, par)

    def vf_copy(slot):
        part = valp.at[1 - side, slot]
        return remote(part, part, sem_fs.at[NPIECE], sem_fr.at[NPIECE], sibling, par)

    def v_arrival():
        part = valp.at[1 - side, core]
        return remote(part, part, sem_ts.at[NPIECE], sem_tr.at[NPIECE], across, par)

    def scatter_copy(snd, rcv, send, recv, i, t):
        dy, dx = offset(i, t)
        slot = dy * NX + dx - 1
        return remote(snd.at[i, t], rcv.at[slot], send.at[slot], recv.at[slot], ex, owner(i, t))

    def scatter(value, i, snd, rcv, send, recv):
        for t in range(NX):
            snd[i, t] = value[:, t * 128 : (t + 1) * 128].astype(jnp.bfloat16)
        for t in range(NX):

            def send_tile():
                scatter_copy(snd, rcv, send, recv, i, t).start()

            if t:
                send_tile()
            else:
                pl.when(i < NY - 1)(send_tile)

    def scatter_wait(snd, rcv, send, recv, d):
        return remote(snd.at[0, 0], rcv.at[d - 1], send.at[d - 1], recv.at[d - 1], ex, (par + d) % NPAR)

    def gathered(snd, rcv, send, recv):
        tile = snd[NY - 1, 0].astype(jnp.float32)
        for dy, dx in [pair for step in ORDER for pair in step if pair != (0, 0)]:
            d = dy * NX + dx
            scatter_wait(snd, rcv, send, recv, d).wait_recv()
            tile += rcv[d - 1].astype(jnp.float32)
        return tile

    pass1 = (snd1, rcv1, ss1, rs1)
    pass2 = (snd2, rcv2, ss2, rs2)

    def z_copy(d):
        peer = (z + 2 * d) % NZ
        part = vall.at[z // 2]
        return remote(part, part, sem_zs.at[d - 1], sem_zr.at[d - 1], peer * 2 + core, par)

    def z_arrival(d):
        source = (z + NZ - 2 * d) % NZ
        part = vall.at[source // 2]
        return remote(part, part, sem_zs.at[d - 1], sem_zr.at[d - 1], source * 2 + core, par)

    def q_copy(n):
        src = (qsend.at[0, 1 - core], qsend.at[1, core], qsend.at[1, 1 - core])[n]
        return remote(src, qrecv.at[n], sem_qs.at[n], sem_qr.at[n], (sibling, across, slant)[n], par)

    def p_copy(d):
        peer = (par + d) % NPAR
        return remote(msg.at[peer], precv.at[d - 1], sem_ps.at[d - 1], sem_pr.at[d - 1], ex, peer)

    def tell(n, neighbours):
        for e, p in neighbours:
            pl.semaphore_signal(sem_ready.at[n], inc=1, device_id=(e, p), device_id_type=MESH)

    def hear(n):
        pl.semaphore_wait(sem_ready.at[n], 2)

    def round_two():
        hear(0)
        tell(1, column)
        hear(3)
        tell(4, stack)

    def round_three():
        hear(1)
        tell(2, column)
        hear(4)
        tell(5, stack)

    def round_four():
        hear(2)
        hear(5)

    def enter():
        arrivals[1].wait()
        val_rows = val_in[...].astype(jnp.float32)
        vpad[core] = jnp.concatenate([val_rows, jnp.zeros_like(val_rows)], axis=0).astype(jnp.bfloat16)
        arrivals[2].wait()
        arrivals[3].wait()
        pl.semaphore_wait(barrier, 7)
        tell(0, row)
        tell(3, stack)
        share_copy(0, vpad, core).start()
        t_copy(0).start()
        share_copy(1, loc, core).start()

    def send_val():
        share_copy(0, vpad, 1 - core).wait_recv()
        own_val = jnp.concatenate(
            [vpad[0].astype(jnp.float32)[:NVA], vpad[1].astype(jnp.float32)[:NVA]], axis=0
        ).astype(jnp.bfloat16)
        valp[side, 0] = own_val[:, :HALF]
        valp[side, 1] = own_val[:, HALF:]
        v_copy().start()

    def forward_val():
        v_arrival().wait_recv()
        vf_copy(core).start()

    def shared():
        vf_copy(1 - core).wait_recv()
        share_copy(1, loc, 1 - core).wait_recv()

    events = {
        1: [enter],
        3: [send_val, lambda: t_copy(1).start()],
        4: [round_two],
        5: [lambda: t_copy(2).start(), lambda: t_copy(3).start()],
        6: [round_three, lambda: forward(0)],
        7: [lambda: t_copy(4).start()],
        8: [lambda: t_copy(5).start(), round_four, forward_val],
        9: [lambda: t_copy(6).start(), lambda: forward(1)],
        10: [lambda: t_copy(7).start(), shared],
        11: [lambda: forward(2), lambda: forward(3)],
        13: [lambda: forward(4)],
        14: [lambda: forward(5)],
        15: [lambda: forward(6)],
    }

    def own_rows(n):
        i = jnp.where(n < 12, n - 10, jnp.where(n < 15, 2, 3))
        scatter(product1(i), i, *pass1)

    def after(n, low, high):
        if not any(low <= when < high for when in events):
            return
        if high - low == 1:
            for thing in events[low]:
                thing()
            return
        middle = (low + high) // 2

        @pl.when(n < middle)
        def _():
            after(n, low, middle)

        @pl.when(n >= middle)
        def _():
            after(n, middle, high)

    @pl.loop(0, NY * NB)
    def _(n):
        make_signs(n)
        after(n, 0, NY * NB)

        @pl.when((n == 10) | (n == 11) | (n == 12) | (n == 15))
        def _():
            own_rows(n)

    forward(7)

    for k in range(NPIECE):
        f_copy(k, 1 - core).wait_recv()

    @pl.loop(0, NY)
    def _(i):
        scatter(product2(i), i, *pass2)

    first = gathered(*pass1)
    vall[z // 2] = (first[2 * NTR :] * ROOT).astype(jnp.bfloat16)
    for d in range(1, NZ // 2):
        z_copy(d).start()

    lane = lax.broadcasted_iota(jnp.int32, (128, 128), 1)
    row = lax.broadcasted_iota(jnp.int32, (128, 128), 0)
    ones = jnp.ones((128, 128), jnp.bfloat16)

    for d in range(1, NZ // 2):
        z_arrival(d).wait_recv()
    values = vall[...].reshape(128, 128)
    square = values.astype(jnp.float32)
    val_sq = split_dot(square * square, ones, 0)

    def products(rows, chip):
        rows = rows * (ROOT / 512.0)
        inner = dot_t(values, rows.astype(jnp.bfloat16))
        train_sq = pltpu.roll(split_dot(ones, rows * rows, 1), NTR, 1)
        sums = jnp.where(
            lane % 8 == row % 8,
            train_sq,
            jnp.where(lane % 8 == (row + 1) % 8, val_sq, 0.0),
        )
        pair = jnp.where(lane < NTR, inner, sums), jnp.where(lane < NTR, sums, inner)
        qsend[chip, 0] = pair[0].astype(jnp.bfloat16)
        qsend[chip, 1] = pair[1].astype(jnp.bfloat16)

    products(first[: 2 * NTR], 0)
    q_copy(0).start()
    products(gathered(*pass2), 1)
    q_copy(1).start()
    q_copy(2).start()
    whole = qsend[0, core].astype(jnp.float32)
    for n in range(3):
        q_copy(n).wait_recv()
        whole += qrecv[n].astype(jnp.float32)
    msg[...] = whole.reshape(NPAR, 8, 128)
    for d in range(1, NPAR):
        p_copy(d).start()

    for n, ref in enumerate((vpad, loc)):
        share_copy(n, ref, core).wait_send()
    for k in range(NPIECE):
        t_copy(k).wait_send()
        f_copy(k, core).wait_send()
    v_copy().wait_send()
    vf_copy(core).wait_send()
    for d in range(1, NPAR):
        for group in (pass1, pass2):
            scatter_wait(*group, d).wait_send()
    for d in range(1, NZ // 2):
        z_copy(d).wait_send()
    for n in range(3):
        q_copy(n).wait_send()
    for d in range(1, NPAR):
        p_copy(d).wait_recv()
    result = msg[par]
    for d in range(1, NPAR):
        result += precv[d - 1]
    result = jnp.where(core == 1, pltpu.roll(result, NTR, 1), result)

    lane8 = lax.broadcasted_iota(jnp.int32, (8, 128), 1)
    row8 = lax.broadcasted_iota(jnp.int32, (8, 128), 0)
    train_sq = jnp.sum(jnp.where(lane8 % 8 == row8, result, 0.0), axis=0, keepdims=True)[:, NTR:]
    val_sq = 0.125 * jnp.sum(
        jnp.where((lane8 >= NTR) & (lane8 % 8 == (row8 + 1) % 8), result, 0.0), axis=1, keepdims=True
    )
    back = 512.0 / tokens[...].astype(jnp.float32)
    train_norm = jnp.sqrt(train_sq * back * back + 1e-6)
    val_norm = jnp.sqrt(val_sq + 1e-6)
    norm_ref[...] = train_norm
    scores = result[:, :NTR] * back / (train_norm * val_norm)
    scores_ref[...] = scores.T

    for d in range(1, NPAR):
        p_copy(d).wait_send()


def local(train_grads, val_grads, token_counts, proj_salt):
    vmem = pl.BlockSpec(memory_space=pltpu.VMEM)
    dma = pltpu.SemaphoreType.DMA
    bf16, f32 = jnp.bfloat16, jnp.float32
    scores, norm = pl.pallas_call(
        kernel,
        out_shape=(
            jax.ShapeDtypeStruct((NTR, NVA), f32),
            jax.ShapeDtypeStruct((1, NTR), f32),
        ),
        in_specs=[pl.BlockSpec(memory_space=pltpu.HBM)] * 4,
        out_specs=(vmem, vmem),
        scratch_shapes=[
            pltpu.SMEM((1,), jnp.int32),
            pltpu.VMEM((1, NTR), jnp.int32),
            pltpu.VMEM((NVA, PD), bf16),
            pltpu.VMEM((2, NTR, PD), bf16),
            pltpu.VMEM((2, NTR, PD), bf16),
            pltpu.VMEM((2, 2 * NVA, PD), bf16),
            pltpu.VMEM((2, 2, 2 * NVA, PD // 2), bf16),
            pltpu.VMEM((NY, PD, KB), bf16),
            pltpu.VMEM((NY, NX, R1, 128), bf16),
            pltpu.VMEM((NY, NX, R2, 128), bf16),
            pltpu.VMEM((NPAR - 1, R1, 128), bf16),
            pltpu.VMEM((NPAR - 1, R2, 128), bf16),
            pltpu.VMEM((NZ // 2, 4 * NVA, 128), bf16),
            pltpu.VMEM((2, 2, 128, 128), bf16),
            pltpu.VMEM((3, 128, 128), bf16),
            pltpu.VMEM((NPAR, 8, 128), f32),
            pltpu.VMEM((NPAR - 1, 8, 128), f32),
            pltpu.SemaphoreType.REGULAR((6,)),
            dma((4,)),
            dma((4,)),
            dma((NPIECE + 1,)),
            dma((NPIECE + 1,)),
            dma((NPIECE + 1,)),
            dma((NPIECE + 1,)),
            dma((NPAR - 1,)),
            dma((NPAR - 1,)),
            dma((NPAR - 1,)),
            dma((NPAR - 1,)),
            dma((NZ // 2 - 1,)),
            dma((NZ // 2 - 1,)),
            dma((3,)),
            dma((3,)),
            dma((NPAR - 1,)),
            dma((NPAR - 1,)),
        ],
        compiler_params=pltpu.CompilerParams(
            collective_id=0, has_side_effects=True, vmem_limit_bytes=52 * 2**20
        ),
    )(proj_salt, train_grads, val_grads, token_counts.reshape(1, NTR))
    return scores, norm.reshape(NTR)


def solution(mesh):
    placed = (P("ex", "par"), P("ex", "par"), P("ex"), P())
    return jax.shard_map(
        local, mesh=mesh, in_specs=placed, out_specs=(P("ex", "par"), P("ex")), check_vma=False
    )
```

```python
import jax
import jax.numpy as jnp
from jax import lax
from jax.experimental import pallas as pl
from jax.experimental.pallas import tpu as pltpu
from jax.sharding import PartitionSpec as P

K = 8192
C1, C2, C3, CS = 625341585, 739982445, 695872825, 461845907
MESH = pl.DeviceIdType.MESH
NX = 4
NY = 4
NPAR = NX * NY
NZ = 8
NTR = 64
NVA = 8
PD = 4096
KQ = K // 4
KB = 512
QB = 1024
NB = PD // QB
NPIECE = 8
QP = PD // NPIECE
HALF = PD // 2
R1, R2 = 2 * NTR + 4 * NVA, 2 * NTR
SLAB = 16
UNROLL = 64
ROOT = 1.0 / K**0.5
ORDER = (
    ((2, 2), (1, 2), (3, 2), (2, 0)),
    ((2, 1), (2, 3), (0, 2), (1, 1)),
    ((3, 3), (1, 3), (3, 1), (0, 1)),
    ((0, 0), (0, 3), (1, 0), (3, 0)),
)


def wrap(value):
    value &= 0xFFFFFFFF
    return value - (1 << 32) if value >= (1 << 31) else value


def srl(value, amount):
    return lax.shift_right_logical(value, jnp.full_like(value, amount))


def signs_of(value):
    value = value ^ srl(value, 15)
    value = value * C2
    value = value ^ srl(value, 12)
    value = value * C3
    value = value ^ (value << 15)
    return jnp.where(value < 0, jnp.bfloat16(-1.0), jnp.bfloat16(1.0))


def dot_t(a, b):
    return lax.dot_general(a, b, (((1,), (1,)), ((), ())), preferred_element_type=jnp.float32)


def split_dot(a, b, exact):
    pair = (a, b)
    high = pair[exact].astype(jnp.bfloat16)
    low = (pair[exact] - high.astype(jnp.float32)).astype(jnp.bfloat16)
    if exact == 0:
        return dot_t(high, b) + dot_t(low, b)
    return dot_t(a, high) + dot_t(a, low)


def kernel(
    salt_ref, train_ref, val_ref, tokens_ref, scores_ref, norm_ref,
    salt, tokens, val_in, loc, rem, vpad, valp, signs,
    snd1, snd2, rcv1, rcv2,
    vall, qsend, qrecv, msg, precv,
    sem_ready, sem_in, sem_share, sem_ts, sem_tr, sem_fs, sem_fr,
    ss1, rs1, ss2, rs2, sem_zs, sem_zr, sem_qs, sem_qr, sem_ps, sem_pr,
):
    ex = lax.axis_index("ex")
    par = lax.axis_index("par")
    z, core = ex // 2, ex % 2
    y, x = par // NX, par % NX
    side = z % 2
    partner = z + 1 - 2 * side
    sibling = z * 2 + (1 - core)
    across = partner * 2 + core
    slant = partner * 2 + (1 - core)

    arrivals = [
        pltpu.make_async_copy(src, dst, sem_in.at[n])
        for n, (src, dst) in enumerate(
            ((salt_ref, salt), (val_ref, val_in), (train_ref, loc.at[core]), (tokens_ref, tokens))
        )
    ]
    for arrival in arrivals:
        arrival.start()

    barrier = pltpu.get_barrier_semaphore()

    def greet(e, p):
        pl.semaphore_signal(barrier, inc=1, device_id=(e, p), device_id_type=MESH)

    row = [(ex, y * NX + (x + d) % NX) for d in (1, NX - 1)]
    column = [(ex, ((y + d) % NY) * NX + x) for d in (1, NY - 1)]
    stack = [(((z + d) % NZ) * 2 + core, par) for d in (1, NZ - 1)]
    greet(sibling, par)
    for e, p in stack + row + column:
        greet(e, p)


    arrivals[0].wait()
    base = (
        salt[0] * CS
        + par * wrap(PD * K * C1)
        + (side * 2 + core) * wrap(KQ * C1)
    )
    grid0 = (
        lax.broadcasted_iota(jnp.int32, (SLAB, 128), 0) * K
        + lax.broadcasted_iota(jnp.int32, (SLAB, 128), 1)
    ) * C1

    def offset(i, t):
        def pick(axis):
            value = ORDER[NY - 1][t][axis]
            for j in range(NY - 1):
                value = jnp.where(i == j, ORDER[j][t][axis], value)
            return value

        return pick(0), pick(1)

    def owner(i, t):
        dy, dx = offset(i, t)
        return ((y + dy) % NY) * NX + (x + dx) % NX

    def make_signs(n):
        i, b = n // NB, n % NB
        start = base + b * wrap(QB * K * C1)
        grid = jnp.concatenate([grid0 + (start + owner(i, t) * wrap(128 * C1)) for t in range(NX)], axis=1)

        @pl.loop(0, QB // (UNROLL * SLAB))
        def _(v):
            here = v * wrap(UNROLL * SLAB * K * C1)
            for u in range(UNROLL):
                at = pl.multiple_of(b * QB + (v * UNROLL + u) * SLAB, SLAB)
                signs[i, pl.ds(at, SLAB), :] = signs_of(grid + (here + wrap(u * SLAB * K * C1)))

    def product1(i):
        values = [valp[:, h].reshape(4 * NVA, HALF) for h in range(2)]
        rows = jnp.concatenate([loc[...].reshape(2 * NTR, PD), jnp.concatenate(values, axis=1)], axis=0)
        return jnp.dot(rows, signs[i], preferred_element_type=jnp.float32)

    def product2(i):
        return jnp.dot(rem[...].reshape(R2, PD), signs[i], preferred_element_type=jnp.float32)

    def remote(src, dst, send, recv, e, p):
        return pltpu.make_async_remote_copy(
            src_ref=src, dst_ref=dst, send_sem=send, recv_sem=recv,
            device_id=(e, p), device_id_type=MESH,
        )

    def share_copy(n, ref, slot):
        return remote(ref.at[slot], ref.at[slot], sem_share.at[n], sem_share.at[n + 2], sibling, par)

    def t_copy(k):
        part = slice(k * QP, (k + 1) * QP)
        return remote(
            loc.at[core, :, part], rem.at[core, :, part], sem_ts.at[k], sem_tr.at[k], across, par
        )

    def f_copy(k, slot):
        part = rem.at[slot, :, k * QP : (k + 1) * QP]
        return remote(part, part, sem_fs.at[k], sem_fr.at[k], sibling, par)

    def forward(k):
        t_copy(k).wait_recv()
        f_copy(k, core).start()

    def v_copy():
        part = valp.at[side, core]
        return remote(part, part, sem_ts.at[NPIECE], sem_tr.at[NPIECE], across, par)

    def vf_copy(slot):
        part = valp.at[1 - side, slot]
        return remote(part, part, sem_fs.at[NPIECE], sem_fr.at[NPIECE], sibling, par)

    def v_arrival():
        part = valp.at[1 - side, core]
        return remote(part, part, sem_ts.at[NPIECE], sem_tr.at[NPIECE], across, par)

    def scatter_copy(snd, rcv, send, recv, i, t):
        dy, dx = offset(i, t)
        slot = dy * NX + dx - 1
        return remote(snd.at[i, t], rcv.at[slot], send.at[slot], recv.at[slot], ex, owner(i, t))

    def scatter(value, i, snd, rcv, send, recv):
        for t in range(NX):
            snd[i, t] = value[:, t * 128 : (t + 1) * 128].astype(jnp.bfloat16)
        for t in range(NX):

            def send_tile():
                scatter_copy(snd, rcv, send, recv, i, t).start()

            if t:
                send_tile()
            else:
                pl.when(i < NY - 1)(send_tile)

    def scatter_wait(snd, rcv, send, recv, d):
        return remote(snd.at[0, 0], rcv.at[d - 1], send.at[d - 1], recv.at[d - 1], ex, (par + d) % NPAR)

    def gathered(snd, rcv, send, recv):
        tile = snd[NY - 1, 0].astype(jnp.float32)
        for dy, dx in [pair for step in ORDER for pair in step if pair != (0, 0)]:
            d = dy * NX + dx
            scatter_wait(snd, rcv, send, recv, d).wait_recv()
            tile += rcv[d - 1].astype(jnp.float32)
        return tile

    pass1 = (snd1, rcv1, ss1, rs1)
    pass2 = (snd2, rcv2, ss2, rs2)

    def z_copy(d):
        peer = (z + 2 * d) % NZ
        part = vall.at[z // 2]
        return remote(part, part, sem_zs.at[d - 1], sem_zr.at[d - 1], peer * 2 + core, par)

    def z_arrival(d):
        source = (z + NZ - 2 * d) % NZ
        part = vall.at[source // 2]
        return remote(part, part, sem_zs.at[d - 1], sem_zr.at[d - 1], source * 2 + core, par)

    def q_copy(n):
        src = (qsend.at[0, 1 - core], qsend.at[1, core], qsend.at[1, 1 - core])[n]
        return remote(src, qrecv.at[n], sem_qs.at[n], sem_qr.at[n], (sibling, across, slant)[n], par)

    far_first = [dy * NX + dx for step in ORDER for dy, dx in step if (dy, dx) != (0, 0)]

    def p_copy(d):
        peer = ((y + d // NX) % NY) * NX + (x + d % NX) % NX
        return remote(msg.at[peer], precv.at[d - 1], sem_ps.at[d - 1], sem_pr.at[d - 1], ex, peer)

    def tell(n, neighbours):
        for e, p in neighbours:
            pl.semaphore_signal(sem_ready.at[n], inc=1, device_id=(e, p), device_id_type=MESH)

    def hear(n):
        pl.semaphore_wait(sem_ready.at[n], 2)

    def round_two():
        hear(0)
        tell(1, column)
        hear(3)
        tell(4, stack)

    def round_three():
        hear(1)
        tell(2, column)
        hear(4)
        tell(5, stack)

    def round_four():
        hear(2)
        hear(5)

    def enter():
        arrivals[1].wait()
        val_rows = val_in[...].astype(jnp.float32)
        vpad[core] = jnp.concatenate([val_rows, jnp.zeros_like(val_rows)], axis=0).astype(jnp.bfloat16)
        arrivals[2].wait()
        arrivals[3].wait()
        pl.semaphore_wait(barrier, 7)
        tell(0, row)
        tell(3, stack)
        share_copy(0, vpad, core).start()
        t_copy(0).start()
        share_copy(1, loc, core).start()

    def send_val():
        share_copy(0, vpad, 1 - core).wait_recv()
        own_val = jnp.concatenate(
            [vpad[0].astype(jnp.float32)[:NVA], vpad[1].astype(jnp.float32)[:NVA]], axis=0
        ).astype(jnp.bfloat16)
        valp[side, 0] = own_val[:, :HALF]
        valp[side, 1] = own_val[:, HALF:]
        v_copy().start()

    def forward_val():
        v_arrival().wait_recv()
        vf_copy(core).start()

    def shared():
        vf_copy(1 - core).wait_recv()
        share_copy(1, loc, 1 - core).wait_recv()

    events = {
        1: [enter],
        3: [send_val, lambda: t_copy(1).start()],
        4: [round_two],
        5: [lambda: t_copy(2).start(), lambda: t_copy(3).start()],
        6: [round_three, lambda: forward(0)],
        7: [lambda: t_copy(4).start()],
        8: [lambda: t_copy(5).start(), round_four, forward_val],
        9: [lambda: t_copy(6).start(), lambda: forward(1)],
        10: [lambda: t_copy(7).start(), shared],
        11: [lambda: forward(2), lambda: forward(3)],
        13: [lambda: forward(4)],
        14: [lambda: forward(5)],
        15: [lambda: forward(6), lambda: forward(7)],
    }

    def own_rows(n):
        i = jnp.where(n < 12, n - 10, jnp.where(n < 15, 2, 3))
        scatter(product1(i), i, *pass1)

    def after(n, low, high):
        if not any(low <= when < high for when in events):
            return
        if high - low == 1:
            for thing in events[low]:
                thing()
            return
        middle = (low + high) // 2

        @pl.when(n < middle)
        def _():
            after(n, low, middle)

        @pl.when(n >= middle)
        def _():
            after(n, middle, high)

    @pl.loop(0, NY * NB)
    def _(n):
        make_signs(n)
        after(n, 0, NY * NB)

        @pl.when((n == 10) | (n == 11) | (n == 12) | (n == 15))
        def _():
            own_rows(n)


    for k in range(NPIECE):
        f_copy(k, 1 - core).wait_recv()

    @pl.loop(0, NY)
    def _(i):
        scatter(product2(i), i, *pass2)

    first = gathered(*pass1)
    vall[z // 2] = (first[2 * NTR :] * ROOT).astype(jnp.bfloat16)
    for d in range(1, NZ // 2):
        z_copy(d).start()

    lane = lax.broadcasted_iota(jnp.int32, (128, 128), 1)
    row = lax.broadcasted_iota(jnp.int32, (128, 128), 0)
    ones = jnp.ones((128, 128), jnp.bfloat16)

    for d in range(1, NZ // 2):
        z_arrival(d).wait_recv()
    values = vall[...].reshape(128, 128)
    square = values.astype(jnp.float32)
    val_sq = split_dot(square * square, ones, 0)

    def products(rows, chip):
        rows = rows * (ROOT / 512.0)
        inner = dot_t(values, rows.astype(jnp.bfloat16))
        train_sq = pltpu.roll(split_dot(ones, rows * rows, 1), NTR, 1)
        sums = jnp.where(
            lane % 8 == row % 8,
            train_sq,
            jnp.where(lane % 8 == (row + 1) % 8, val_sq, 0.0),
        )
        pair = jnp.where(lane < NTR, inner, sums), jnp.where(lane < NTR, sums, inner)
        qsend[chip, 0] = pair[0].astype(jnp.bfloat16)
        qsend[chip, 1] = pair[1].astype(jnp.bfloat16)

    products(first[: 2 * NTR], 0)
    q_copy(0).start()
    products(gathered(*pass2), 1)
    q_copy(1).start()
    q_copy(2).start()
    whole = qsend[0, core].astype(jnp.float32)
    for n in range(3):
        q_copy(n).wait_recv()
        whole += qrecv[n].astype(jnp.float32)
    msg[...] = whole.reshape(NPAR, 8, 128)
    for d in far_first:
        p_copy(d).start()

    for n, ref in enumerate((vpad, loc)):
        share_copy(n, ref, core).wait_send()
    for k in range(NPIECE):
        t_copy(k).wait_send()
        f_copy(k, core).wait_send()
    v_copy().wait_send()
    vf_copy(core).wait_send()
    for d in range(1, NPAR):
        for group in (pass1, pass2):
            scatter_wait(*group, d).wait_send()
    for d in range(1, NZ // 2):
        z_copy(d).wait_send()
    for n in range(3):
        q_copy(n).wait_send()
    for d in range(1, NPAR):
        p_copy(d).wait_recv()
    result = msg[par]
    for d in range(1, NPAR):
        result += precv[d - 1]
    result = jnp.where(core == 1, pltpu.roll(result, NTR, 1), result)

    lane8 = lax.broadcasted_iota(jnp.int32, (8, 128), 1)
    row8 = lax.broadcasted_iota(jnp.int32, (8, 128), 0)
    train_sq = jnp.sum(jnp.where(lane8 % 8 == row8, result, 0.0), axis=0, keepdims=True)[:, NTR:]
    val_sq = 0.125 * jnp.sum(
        jnp.where((lane8 >= NTR) & (lane8 % 8 == (row8 + 1) % 8), result, 0.0), axis=1, keepdims=True
    )
    back = 512.0 / tokens[...].astype(jnp.float32)
    train_norm = jnp.sqrt(train_sq * back * back + 1e-6)
    val_norm = jnp.sqrt(val_sq + 1e-6)
    norm_ref[...] = train_norm
    scores = result[:, :NTR] * back / (train_norm * val_norm)
    scores_ref[...] = scores

    for d in range(1, NPAR):
        p_copy(d).wait_send()


def local(train_grads, val_grads, token_counts, proj_salt):
    vmem = pl.BlockSpec(memory_space=pltpu.VMEM)
    dma = pltpu.SemaphoreType.DMA
    bf16, f32 = jnp.bfloat16, jnp.float32
    scores, norm = pl.pallas_call(
        kernel,
        out_shape=(
            jax.ShapeDtypeStruct((NVA, NTR), f32),
            jax.ShapeDtypeStruct((1, NTR), f32),
        ),
        in_specs=[pl.BlockSpec(memory_space=pltpu.HBM)] * 4,
        out_specs=(vmem, vmem),
        scratch_shapes=[
            pltpu.SMEM((1,), jnp.int32),
            pltpu.VMEM((1, NTR), jnp.int32),
            pltpu.VMEM((NVA, PD), bf16),
            pltpu.VMEM((2, NTR, PD), bf16),
            pltpu.VMEM((2, NTR, PD), bf16),
            pltpu.VMEM((2, 2 * NVA, PD), bf16),
            pltpu.VMEM((2, 2, 2 * NVA, PD // 2), bf16),
            pltpu.VMEM((NY, PD, KB), bf16),
            pltpu.VMEM((NY, NX, R1, 128), bf16),
            pltpu.VMEM((NY, NX, R2, 128), bf16),
            pltpu.VMEM((NPAR - 1, R1, 128), bf16),
            pltpu.VMEM((NPAR - 1, R2, 128), bf16),
            pltpu.VMEM((NZ // 2, 4 * NVA, 128), bf16),
            pltpu.VMEM((2, 2, 128, 128), bf16),
            pltpu.VMEM((3, 128, 128), bf16),
            pltpu.VMEM((NPAR, 8, 128), f32),
            pltpu.VMEM((NPAR - 1, 8, 128), f32),
            pltpu.SemaphoreType.REGULAR((6,)),
            dma((4,)),
            dma((4,)),
            dma((NPIECE + 1,)),
            dma((NPIECE + 1,)),
            dma((NPIECE + 1,)),
            dma((NPIECE + 1,)),
            dma((NPAR - 1,)),
            dma((NPAR - 1,)),
            dma((NPAR - 1,)),
            dma((NPAR - 1,)),
            dma((NZ // 2 - 1,)),
            dma((NZ // 2 - 1,)),
            dma((3,)),
            dma((3,)),
            dma((NPAR - 1,)),
            dma((NPAR - 1,)),
        ],
        compiler_params=pltpu.CompilerParams(
            collective_id=0, has_side_effects=True, vmem_limit_bytes=52 * 2**20
        ),
    )(proj_salt, train_grads, val_grads, token_counts.reshape(1, NTR))
    return scores.T, norm.reshape(NTR)


def solution(mesh):
    placed = (P("ex", "par"), P("ex", "par"), P("ex"), P())
    return jax.shard_map(
        local, mesh=mesh, in_specs=placed, out_specs=(P("ex", "par"), P("ex")), check_vma=False
    )
```

```python
import jax
import jax.numpy as jnp
from jax import lax
from jax.experimental import pallas as pl
from jax.experimental.pallas import tpu as pltpu
from jax.sharding import PartitionSpec as P

K = 8192
C1, C2, C3, CS = 625341585, 739982445, 695872825, 461845907
MESH = pl.DeviceIdType.MESH
NX = 4
NY = 4
NPAR = NX * NY
NZ = 8
NTR = 64
NVA = 8
PD = 4096
KQ = K // 4
KB = 512
QB = 1024
NB = PD // QB
NPIECE = 8
QP = PD // NPIECE
HALF = PD // 2
R1, R2 = 2 * NTR + 4 * NVA, 2 * NTR
SLAB = 16
UNROLL = 64
ROOT = 1.0 / K**0.5
ORDER = (
    ((2, 2), (1, 2), (3, 2), (2, 0)),
    ((2, 1), (2, 3), (0, 2), (1, 1)),
    ((3, 3), (1, 3), (3, 1), (0, 1)),
    ((0, 0), (0, 3), (1, 0), (3, 0)),
)


def wrap(value):
    value &= 0xFFFFFFFF
    return value - (1 << 32) if value >= (1 << 31) else value


def srl(value, amount):
    return lax.shift_right_logical(value, jnp.full_like(value, amount))


def signs_of(value):
    value = value ^ srl(value, 15)
    value = value * C2
    value = value ^ srl(value, 12)
    value = value * C3
    value = value ^ (value << 15)
    return jnp.where(value < 0, jnp.bfloat16(-1.0), jnp.bfloat16(1.0))


def dot_t(a, b):
    return lax.dot_general(a, b, (((1,), (1,)), ((), ())), preferred_element_type=jnp.float32)


def split_dot(a, b, exact):
    pair = (a, b)
    high = pair[exact].astype(jnp.bfloat16)
    low = (pair[exact] - high.astype(jnp.float32)).astype(jnp.bfloat16)
    if exact == 0:
        return dot_t(high, b) + dot_t(low, b)
    return dot_t(a, high) + dot_t(a, low)


def kernel(
    salt_ref, train_ref, val_ref, tokens_ref, scores_ref, norm_ref,
    salt, tokens, val_in, loc, rem, vpad, valp, signs,
    snd1, snd2, rcv1, rcv2,
    vall, qsend, qrecv, msg, precv,
    sem_ready, sem_in, sem_share, sem_ts, sem_tr, sem_fs, sem_fr,
    ss1, rs1, ss2, rs2, sem_zs, sem_zr, sem_qs, sem_qr, sem_ps, sem_pr,
):
    ex = lax.axis_index("ex")
    par = lax.axis_index("par")
    z, core = ex // 2, ex % 2
    y, x = par // NX, par % NX
    side = z % 2
    partner = z + 1 - 2 * side
    sibling = z * 2 + (1 - core)
    across = partner * 2 + core
    slant = partner * 2 + (1 - core)

    arrivals = [
        pltpu.make_async_copy(src, dst, sem_in.at[n])
        for n, (src, dst) in enumerate(
            ((salt_ref, salt), (val_ref, val_in), (train_ref, loc.at[core]), (tokens_ref, tokens))
        )
    ]
    for arrival in arrivals:
        arrival.start()

    barrier = pltpu.get_barrier_semaphore()

    def greet(e, p):
        pl.semaphore_signal(barrier, inc=1, device_id=(e, p), device_id_type=MESH)

    row = [(ex, y * NX + (x + d) % NX) for d in (1, NX - 1)]
    column = [(ex, ((y + d) % NY) * NX + x) for d in (1, NY - 1)]
    stack = [(((z + d) % NZ) * 2 + core, par) for d in (1, NZ - 1)]
    greet(sibling, par)
    for e, p in stack + row + column:
        greet(e, p)


    arrivals[0].wait()
    base = (
        salt[0] * CS
        + par * wrap(PD * K * C1)
        + (side * 2 + core) * wrap(KQ * C1)
    )
    grid0 = (
        lax.broadcasted_iota(jnp.int32, (SLAB, 128), 0) * K
        + lax.broadcasted_iota(jnp.int32, (SLAB, 128), 1)
    ) * C1

    def offset(i, t):
        def pick(axis):
            value = ORDER[NY - 1][t][axis]
            for j in range(NY - 1):
                value = jnp.where(i == j, ORDER[j][t][axis], value)
            return value

        return pick(0), pick(1)

    def owner(i, t):
        dy, dx = offset(i, t)
        return ((y + dy) % NY) * NX + (x + dx) % NX

    def make_signs(n):
        i, b = n // NB, n % NB
        start = base + b * wrap(QB * K * C1)
        grid = jnp.concatenate([grid0 + (start + owner(i, t) * wrap(128 * C1)) for t in range(NX)], axis=1)

        @pl.loop(0, QB // (UNROLL * SLAB))
        def _(v):
            here = v * wrap(UNROLL * SLAB * K * C1)
            for u in range(UNROLL):
                at = pl.multiple_of(b * QB + (v * UNROLL + u) * SLAB, SLAB)
                signs[i, pl.ds(at, SLAB), :] = signs_of(grid + (here + wrap(u * SLAB * K * C1)))

    def product1(i):
        values = [valp[:, h].reshape(4 * NVA, HALF) for h in range(2)]
        rows = jnp.concatenate([loc[...].reshape(2 * NTR, PD), jnp.concatenate(values, axis=1)], axis=0)
        return jnp.dot(rows, signs[i], preferred_element_type=jnp.float32)

    def product2(i):
        return jnp.dot(rem[...].reshape(R2, PD), signs[i], preferred_element_type=jnp.float32)

    def remote(src, dst, send, recv, e, p):
        return pltpu.make_async_remote_copy(
            src_ref=src, dst_ref=dst, send_sem=send, recv_sem=recv,
            device_id=(e, p), device_id_type=MESH,
        )

    def share_copy(n, ref, slot):
        return remote(ref.at[slot], ref.at[slot], sem_share.at[n], sem_share.at[n + 2], sibling, par)

    def t_copy(k):
        part = slice(k * QP, (k + 1) * QP)
        return remote(
            loc.at[core, :, part], rem.at[core, :, part], sem_ts.at[k], sem_tr.at[k], across, par
        )

    def f_copy(k, slot):
        part = rem.at[slot, :, k * QP : (k + 1) * QP]
        return remote(part, part, sem_fs.at[k], sem_fr.at[k], sibling, par)

    def forward(k):
        t_copy(k).wait_recv()
        f_copy(k, core).start()

    def v_copy():
        part = valp.at[side, core]
        return remote(part, part, sem_ts.at[NPIECE], sem_tr.at[NPIECE], across, par)

    def vf_copy(slot):
        part = valp.at[1 - side, slot]
        return remote(part, part, sem_fs.at[NPIECE], sem_fr.at[NPIECE], sibling, par)

    def v_arrival():
        part = valp.at[1 - side, core]
        return remote(part, part, sem_ts.at[NPIECE], sem_tr.at[NPIECE], across, par)

    def scatter_copy(snd, rcv, send, recv, i, t):
        dy, dx = offset(i, t)
        slot = dy * NX + dx - 1
        return remote(snd.at[i, t], rcv.at[slot], send.at[slot], recv.at[slot], ex, owner(i, t))

    def scatter(value, i, snd, rcv, send, recv):
        for t in range(NX):
            snd[i, t] = value[:, t * 128 : (t + 1) * 128].astype(jnp.bfloat16)
        for t in range(NX):

            def send_tile():
                scatter_copy(snd, rcv, send, recv, i, t).start()

            if t:
                send_tile()
            else:
                pl.when(i < NY - 1)(send_tile)

    def scatter_wait(snd, rcv, send, recv, d):
        return remote(snd.at[0, 0], rcv.at[d - 1], send.at[d - 1], recv.at[d - 1], ex, (par + d) % NPAR)

    def gathered(snd, rcv, send, recv):
        tile = snd[NY - 1, 0].astype(jnp.float32)
        for dy, dx in [pair for step in ORDER for pair in step if pair != (0, 0)]:
            d = dy * NX + dx
            scatter_wait(snd, rcv, send, recv, d).wait_recv()
            tile += rcv[d - 1].astype(jnp.float32)
        return tile

    pass1 = (snd1, rcv1, ss1, rs1)
    pass2 = (snd2, rcv2, ss2, rs2)

    def z_copy(d):
        peer = (z + 2 * d) % NZ
        part = vall.at[z // 2]
        return remote(part, part, sem_zs.at[d - 1], sem_zr.at[d - 1], peer * 2 + core, par)

    def z_arrival(d):
        source = (z + NZ - 2 * d) % NZ
        part = vall.at[source // 2]
        return remote(part, part, sem_zs.at[d - 1], sem_zr.at[d - 1], source * 2 + core, par)

    def q_copy(n):
        src = (qsend.at[0, 1 - core], qsend.at[1, core], qsend.at[1, 1 - core])[n]
        return remote(src, qrecv.at[n], sem_qs.at[n], sem_qr.at[n], (sibling, across, slant)[n], par)

    far_first = [dy * NX + dx for step in ORDER for dy, dx in step if (dy, dx) != (0, 0)]

    def p_copy(d):
        peer = ((y + d // NX) % NY) * NX + (x + d % NX) % NX
        return remote(msg.at[peer], precv.at[d - 1], sem_ps.at[d - 1], sem_pr.at[d - 1], ex, peer)

    def tell(n, neighbours):
        for e, p in neighbours:
            pl.semaphore_signal(sem_ready.at[n], inc=1, device_id=(e, p), device_id_type=MESH)

    def hear(n):
        pl.semaphore_wait(sem_ready.at[n], 2)

    def round_two():
        hear(0)
        tell(1, column)
        hear(3)
        tell(4, stack)

    def round_three():
        hear(1)
        tell(2, column)
        hear(4)
        tell(5, stack)

    def round_four():
        hear(2)
        hear(5)

    def enter():
        arrivals[1].wait()
        val_rows = val_in[...].astype(jnp.float32)
        vpad[core] = jnp.concatenate([val_rows, jnp.zeros_like(val_rows)], axis=0).astype(jnp.bfloat16)
        arrivals[2].wait()
        arrivals[3].wait()
        pl.semaphore_wait(barrier, 7)
        tell(0, row)
        tell(3, stack)
        share_copy(0, vpad, core).start()
        t_copy(0).start()
        share_copy(1, loc, core).start()

    def send_val():
        share_copy(0, vpad, 1 - core).wait_recv()
        own_val = jnp.concatenate(
            [vpad[0].astype(jnp.float32)[:NVA], vpad[1].astype(jnp.float32)[:NVA]], axis=0
        ).astype(jnp.bfloat16)
        valp[side, 0] = own_val[:, :HALF]
        valp[side, 1] = own_val[:, HALF:]
        v_copy().start()

    def forward_val():
        v_arrival().wait_recv()
        vf_copy(core).start()

    def shared():
        vf_copy(1 - core).wait_recv()
        share_copy(1, loc, 1 - core).wait_recv()

    events = {
        1: [enter],
        3: [send_val, lambda: t_copy(1).start()],
        4: [round_two],
        5: [lambda: t_copy(2).start(), lambda: t_copy(3).start()],
        6: [round_three, lambda: forward(0)],
        7: [lambda: t_copy(4).start()],
        8: [lambda: t_copy(5).start(), round_four, forward_val],
        9: [lambda: t_copy(6).start(), lambda: forward(1)],
        10: [lambda: t_copy(7).start(), shared],
        11: [lambda: forward(2), lambda: forward(3)],
        13: [lambda: forward(4)],
        14: [lambda: forward(5)],
        15: [lambda: forward(6), lambda: forward(7)],
    }

    def own_rows(n):
        i = jnp.where(n < 13, n - 10, jnp.where(n < 15, 2, 3))
        scatter(product1(i), i, *pass1)

    def after(n, low, high):
        if not any(low <= when < high for when in events):
            return
        if high - low == 1:
            for thing in events[low]:
                thing()
            return
        middle = (low + high) // 2

        @pl.when(n < middle)
        def _():
            after(n, low, middle)

        @pl.when(n >= middle)
        def _():
            after(n, middle, high)

    @pl.loop(0, NY * NB)
    def _(n):
        make_signs(n)
        after(n, 0, NY * NB)

        @pl.when((n == 10) | (n == 11) | (n == 13) | (n == 15))
        def _():
            own_rows(n)


    for k in range(NPIECE):
        f_copy(k, 1 - core).wait_recv()

    @pl.loop(0, NY)
    def _(i):
        scatter(product2(i), i, *pass2)

    first = gathered(*pass1)
    vall[z // 2] = (first[2 * NTR :] * ROOT).astype(jnp.bfloat16)
    for d in range(1, NZ // 2):
        z_copy(d).start()

    lane = lax.broadcasted_iota(jnp.int32, (128, 128), 1)
    row = lax.broadcasted_iota(jnp.int32, (128, 128), 0)
    ones = jnp.ones((128, 128), jnp.bfloat16)

    for d in range(1, NZ // 2):
        z_arrival(d).wait_recv()
    values = vall[...].reshape(128, 128)
    square = values.astype(jnp.float32)
    val_sq = split_dot(square * square, ones, 0)

    def products(rows, chip):
        rows = rows * (ROOT / 512.0)
        inner = dot_t(values, rows.astype(jnp.bfloat16))
        train_sq = pltpu.roll(split_dot(ones, rows * rows, 1), NTR, 1)
        sums = jnp.where(
            lane % 8 == row % 8,
            train_sq,
            jnp.where(lane % 8 == (row + 1) % 8, val_sq, 0.0),
        )
        pair = jnp.where(lane < NTR, inner, sums), jnp.where(lane < NTR, sums, inner)
        qsend[chip, 0] = pair[0].astype(jnp.bfloat16)
        qsend[chip, 1] = pair[1].astype(jnp.bfloat16)

    products(first[: 2 * NTR], 0)
    q_copy(0).start()
    products(gathered(*pass2), 1)
    q_copy(1).start()
    q_copy(2).start()
    whole = qsend[0, core].astype(jnp.float32)
    for n in range(3):
        q_copy(n).wait_recv()
        whole += qrecv[n].astype(jnp.float32)
    msg[...] = whole.reshape(NPAR, 8, 128)
    for d in far_first:
        p_copy(d).start()

    for n, ref in enumerate((vpad, loc)):
        share_copy(n, ref, core).wait_send()
    for k in range(NPIECE):
        t_copy(k).wait_send()
        f_copy(k, core).wait_send()
    v_copy().wait_send()
    vf_copy(core).wait_send()
    for d in range(1, NPAR):
        for group in (pass1, pass2):
            scatter_wait(*group, d).wait_send()
    for d in range(1, NZ // 2):
        z_copy(d).wait_send()
    for n in range(3):
        q_copy(n).wait_send()
    for d in range(1, NPAR):
        p_copy(d).wait_recv()
    result = msg[par]
    for d in range(1, NPAR):
        result += precv[d - 1]
    result = jnp.where(core == 1, pltpu.roll(result, NTR, 1), result)

    lane8 = lax.broadcasted_iota(jnp.int32, (8, 128), 1)
    row8 = lax.broadcasted_iota(jnp.int32, (8, 128), 0)
    train_sq = jnp.sum(jnp.where(lane8 % 8 == row8, result, 0.0), axis=0, keepdims=True)[:, NTR:]
    val_sq = 0.125 * jnp.sum(
        jnp.where((lane8 >= NTR) & (lane8 % 8 == (row8 + 1) % 8), result, 0.0), axis=1, keepdims=True
    )
    back = 512.0 / tokens[...].astype(jnp.float32)
    train_norm = jnp.sqrt(train_sq * back * back + 1e-6)
    val_norm = jnp.sqrt(val_sq + 1e-6)
    norm_ref[...] = train_norm
    scores = result[:, :NTR] * back / (train_norm * val_norm)
    scores_ref[...] = scores

    for d in range(1, NPAR):
        p_copy(d).wait_send()


def local(train_grads, val_grads, token_counts, proj_salt):
    vmem = pl.BlockSpec(memory_space=pltpu.VMEM)
    dma = pltpu.SemaphoreType.DMA
    bf16, f32 = jnp.bfloat16, jnp.float32
    scores, norm = pl.pallas_call(
        kernel,
        out_shape=(
            jax.ShapeDtypeStruct((NVA, NTR), f32),
            jax.ShapeDtypeStruct((1, NTR), f32),
        ),
        in_specs=[pl.BlockSpec(memory_space=pltpu.HBM)] * 4,
        out_specs=(vmem, vmem),
        scratch_shapes=[
            pltpu.SMEM((1,), jnp.int32),
            pltpu.VMEM((1, NTR), jnp.int32),
            pltpu.VMEM((NVA, PD), bf16),
            pltpu.VMEM((2, NTR, PD), bf16),
            pltpu.VMEM((2, NTR, PD), bf16),
            pltpu.VMEM((2, 2 * NVA, PD), bf16),
            pltpu.VMEM((2, 2, 2 * NVA, PD // 2), bf16),
            pltpu.VMEM((NY, PD, KB), bf16),
            pltpu.VMEM((NY, NX, R1, 128), bf16),
            pltpu.VMEM((NY, NX, R2, 128), bf16),
            pltpu.VMEM((NPAR - 1, R1, 128), bf16),
            pltpu.VMEM((NPAR - 1, R2, 128), bf16),
            pltpu.VMEM((NZ // 2, 4 * NVA, 128), bf16),
            pltpu.VMEM((2, 2, 128, 128), bf16),
            pltpu.VMEM((3, 128, 128), bf16),
            pltpu.VMEM((NPAR, 8, 128), f32),
            pltpu.VMEM((NPAR - 1, 8, 128), f32),
            pltpu.SemaphoreType.REGULAR((6,)),
            dma((4,)),
            dma((4,)),
            dma((NPIECE + 1,)),
            dma((NPIECE + 1,)),
            dma((NPIECE + 1,)),
            dma((NPIECE + 1,)),
            dma((NPAR - 1,)),
            dma((NPAR - 1,)),
            dma((NPAR - 1,)),
            dma((NPAR - 1,)),
            dma((NZ // 2 - 1,)),
            dma((NZ // 2 - 1,)),
            dma((3,)),
            dma((3,)),
            dma((NPAR - 1,)),
            dma((NPAR - 1,)),
        ],
        compiler_params=pltpu.CompilerParams(
            collective_id=0, has_side_effects=True, vmem_limit_bytes=52 * 2**20
        ),
    )(proj_salt, train_grads, val_grads, token_counts.reshape(1, NTR))
    return scores.T, norm.reshape(NTR)


def solution(mesh):
    placed = (P("ex", "par"), P("ex", "par"), P("ex"), P())
    return jax.shard_map(
        local, mesh=mesh, in_specs=placed, out_specs=(P("ex", "par"), P("ex")), check_vma=False
    )
```
